32 devices in a mesh: member: 2 (over y), gx: 4 (over z), gy: 2 (over x), gz: 2 (over core).
Axes of the slice: x: 2, y: 2, z: 4, core: 2. Of those that a mesh axis runs over, the one named last changes fastest.
Arguments:
- parent: float32 [6, 40, 16, 512], P('member', None, 'gx', ('gy', 'gz')), parts along dimension 0, may hold values from -6 to 6
- nest: float32 [6, 40, 24, 1536], P('member', None, 'gx', ('gy', 'gz')), parts along dimension 0, may hold values from -6 to 6
- nest_anchor: int32 [2], P('member'), parts along dimension 0, may hold values from 4 to 8
- donor_rows: int32 [8, 2, 4, 1536], P('member', None, None, ('gy', 'gz')), parts along dimension 0, may hold values from 0 to 3
- donor_cols: int32 [8, 2, 4, 1536], P('member', None, None, ('gy', 'gz')), parts along dimension 0, may hold values from -1 to 1
- donor_weights: float32 [8, 2, 4, 1536], P('member', None, None, ('gy', 'gz')), parts along dimension 0, may hold values from 0.05 to 0.45
- wind_x: float32 [40], replicated, may hold values from -0.5 to 0.5
- wind_y: float32 [40], replicated, may hold values from -0.5 to 0.5
- column_mix: float32 [40, 40], replicated, may hold values from -0.25 to 0.25
Outputs:
- parent_out: float32 [6, 40, 16, 512], P('member', None, 'gx', ('gy', 'gz')), parts along dimension 0
- nest_out: float32 [6, 40, 24, 1536], P('member', None, 'gx', ('gy', 'gz')), parts along dimension 0
The draws below stay inside these ranges and needn't reach their ends.
There are 2 independent parts, one for each index of `member`. The reference program is written for one: setup_inputs(seed, part) draws one part's arguments, and reference() takes and returns one part's arrays. A program takes and returns all parts, laid end to end along the dimension named above; an argument that names none is the same for every part. Nothing has to cross between parts.
All inputs are finite; a program needn't handle non-finite values.
Results may differ from the reference program's by a relative error of at most 0.0001.
Values sent between devices are 32-bit elements; how exact they have to be, the bound alone decides.
A program may use at most 128 MiB of HBM per device.

```python
import jax
import jax.numpy as jnp
from jax import lax

CXP = 4
LEV = 40
BW = 4
ZR = 4
NXP = 16
NYP = 512
NXN = 24
NYN = 1536


def plant(result, key, least, top_value):
    longest = result.shape.index(max(result.shape))
    spots = []
    for shift in (0, 1):
        where = [jax.random.randint(jax.random.fold_in(key, axis), (), 0, length) for axis, length in enumerate(result.shape)]
        where[longest] = (where[longest] + shift) % result.shape[longest]
        spots.append(tuple(where))
    return result.at[spots[0]].set(least).at[spots[1]].set(top_value)


def block_levels(stream_key, extent, shards, least, high):
    def one(position, parts):
        draws = jax.random.uniform(jax.random.fold_in(jax.random.fold_in(stream_key, 6), position), (parts,), jnp.float32, least / len(shards), high / len(shards))
        return jnp.repeat(jnp.exp(draws), extent[position] // parts).reshape((-1,) + (1,) * (len(extent) - position - 1))

    gain = one(*shards[0])
    for cut in shards[1:]:
        gain = gain * one(*cut)
    return gain


def bell_draw(key, dims, spread, most, cuts=(), kind=jnp.bfloat16):
    entries = spread * jax.random.normal(key, dims, jnp.float32)
    if cuts:
        entries = entries * block_levels(key, dims, cuts, -0.22, 0.18)
    return jnp.clip(entries, -most, most).astype(kind)


def setup_inputs(seed: int = 0, part: int = 0) -> dict:
    seeds = jax.random.split(jax.random.key(seed), 10)
    own_keys = jax.random.split(jax.random.fold_in(seeds[9], part), 10)
    return {
        "parent": bell_draw(own_keys[0], (3, LEV, NXP, NYP), 1.0, 6.0, ((2, 4), (3, 4)), jnp.float32),
        "nest": bell_draw(own_keys[1], (3, LEV, NXN, NYN), 1.0, 6.0, ((2, 4), (3, 4)), jnp.float32),
        "nest_anchor": jax.random.randint(own_keys[2], (1,), CXP, NXP // 2 + 1).astype(jnp.int32),
        "donor_rows": plant(jax.random.randint(own_keys[3], (4, 2, BW, NYN), 0, ZR), jax.random.fold_in(own_keys[3], 1), 0, ZR - 1).astype(jnp.int32),
        "donor_cols": plant(jax.random.randint(own_keys[4], (4, 2, BW, NYN), -1, 2), jax.random.fold_in(own_keys[4], 1), -1, 1).astype(jnp.int32),
        "donor_weights": jnp.clip(0.05 + 0.39999999 * jax.random.uniform(own_keys[5], (4, 2, BW, NYN), jnp.float32) ** block_levels(own_keys[5], (4, 2, BW, NYN), ((3, 4),), -0.2, 0.2), 0.05, 0.45),
        "wind_x": jnp.clip(jax.random.uniform(seeds[6], (LEV,), jnp.float32, -0.5, 0.5), -0.5, 0.5),
        "wind_y": jnp.clip(jax.random.uniform(seeds[7], (LEV,), jnp.float32, -0.5, 0.5), -0.5, 0.5),
        "column_mix": bell_draw(seeds[8], (LEV, LEV), (16 * LEV) ** -0.5, 0.25, (), jnp.float32),
    }


SOUND = 0.6
DIFFUSE = 0.125


def step_padded(padded, wind_x, wind_y, column_mix):
    centre = padded[:, :, 1:-1, 1:-1]
    east_side = padded[:, :, 2:, 1:-1]
    west_side = padded[:, :, :-2, 1:-1]
    north_side = padded[:, :, 1:-1, 2:]
    south_side = padded[:, :, 1:-1, :-2]
    courant_x = wind_x[None, :, None, None]
    courant_y = wind_y[None, :, None, None]
    advected = (centre - 0.5 * courant_x * (east_side - west_side) - 0.5 * courant_y * (north_side - south_side)
                + DIFFUSE * (east_side + west_side + north_side + south_side - 4.0 * centre))
    speed_u = advected[0] - 0.5 * SOUND * (east_side[2] - west_side[2])
    speed_v = advected[1] - 0.5 * SOUND * (north_side[2] - south_side[2])
    pressure = advected[2] - 0.5 * SOUND * ((east_side[0] - west_side[0]) + (north_side[1] - south_side[1]))
    fields = jnp.stack([speed_u, speed_v, pressure])
    return fields + jnp.einsum("lm,kmxy->klxy", column_mix, fields, precision=lax.Precision.HIGHEST)


def pad_both(state):
    return jnp.pad(state, ((0, 0), (0, 0), (1, 1), (1, 1)))


def sample_zone(zone_rows, donor_rows, donor_cols, donor_weights):
    zone_width = zone_rows.shape[-1]
    half_rows = zone_rows.shape[-2] // 2
    nest_cols = donor_rows.shape[-1]
    col_index = jnp.arange(nest_cols, dtype=jnp.int32)[None, None, None, :] // 3 + donor_cols + 1
    edge_index = jnp.arange(2, dtype=jnp.int32)[None, :, None, None]
    flat_index = (edge_index * half_rows + donor_rows) * zone_width + col_index
    flattened = zone_rows.reshape(zone_rows.shape[:-2] + (zone_rows.shape[-2] * zone_width,))
    picked = jnp.take(flattened, flat_index, axis=-1)
    return jnp.sum(picked * donor_weights, axis=-4)


def edge_zone(parent_grid, anchor):
    padded = jnp.pad(parent_grid, ((0, 0), (0, 0), (0, 0), (1, 1)))
    half_span = parent_grid.shape[2] // 2
    west_rows = lax.dynamic_slice_in_dim(padded, anchor, ZR, 2)
    east_rows = lax.dynamic_slice_in_dim(padded, anchor + half_span - ZR, ZR, 2)
    return jnp.concatenate([west_rows, east_rows], axis=2)


def reference(parent, nest, nest_anchor, donor_rows, donor_cols, donor_weights, wind_x, wind_y, column_mix):
    anchor = nest_anchor[0]
    parent_new = step_padded(pad_both(parent), wind_x, wind_y, column_mix)
    zone_rows = jnp.stack([edge_zone(parent, anchor), edge_zone(parent_new, anchor)])
    bounds = sample_zone(zone_rows, donor_rows, donor_cols, donor_weights)
    nest_state = nest
    for substep in range(1, 4):
        nest_state = step_padded(pad_both(nest_state), wind_x, wind_y, column_mix)
        fraction = substep / 3.0
        blended = (1.0 - fraction) * bounds[0] + fraction * bounds[1]
        nest_state = nest_state.at[:, :, :BW].set(blended[:, :, 0])
        nest_state = nest_state.at[:, :, NXN - BW:].set(blended[:, :, 1])
    coarse = nest_state.reshape(3, LEV, NXN // 3, 3, NYN // 3, 3).mean(axis=(3, 5))
    interior = coarse[:, :, 1:-1]
    placed = lax.dynamic_update_slice_in_dim(jnp.zeros_like(parent_new), interior, anchor + 1, 2)
    row_index = jnp.arange(NXP, dtype=jnp.int32)
    inside = (row_index >= anchor + 1) & (row_index < anchor + NXP // 2 - 1)
    parent_out = jnp.where(inside[None, None, :, None], placed, parent_new)
    return parent_out, nest_state
```

```python
import functools

import jax
import jax.numpy as jnp
from jax import lax
from jax.experimental import pallas as pl
from jax.experimental.pallas import tpu as pltpu
from jax.sharding import PartitionSpec as P

MESH = pl.DeviceIdType.MESH
F32 = jnp.float32
BF16 = jnp.bfloat16
T = 128
H = 3
WEST, EAST = 0, 1


def lanes(shape, dim=1):
    return lax.broadcasted_iota(jnp.int32, shape, dim)


def split(x):
    hi = x.astype(BF16)
    lo = (x - hi.astype(F32)).astype(BF16)
    return hi, lo


def kernel(
    X, Y, CY,
    parent, nest, anchor, d_rows, d_cols, d_wts, coef, mixer,
    parent_out, nest_out,
    edge, pb, phb, hl, hh, px, sa, sb, send_w, recv_w, zb, zn, grid, wx, wrb, wxb, b0, b1, co, cb,
    pack_ss, pack_rs, ph_ss, ph_rs, halo_ss, halo_rs, win_ss, win_rs, wt_ss, wt_rs, co_ss, co_rs,
):
    R = parent.shape[1]
    N = nest.shape[1]
    LEV = nest.shape[2]
    C = nest.shape[3]
    W = C + T
    me = lax.axis_index("member")
    ix = lax.axis_index("gx")
    iy = lax.axis_index("gy") * CY + lax.axis_index("gz")
    half = X // 2
    is_west = ix == 0
    is_east = ix == X - 1
    has_col = (iy > 0, iy < Y - 1)

    def dev(x, y):
        return (me, x, y // CY, lax.rem(y, CY))

    def rcopy(src, dst, ss, rs, x, y):
        return pltpu.make_async_remote_copy(
            src_ref=src, dst_ref=dst, send_sem=ss, recv_sem=rs, device_id=dev(x, y), device_id_type=MESH
        )

    def arrived(ref, rs):
        rcopy(ref, ref, halo_ss.at[0], rs, lax.rem(ix + 1, X), iy).wait_recv()

    def col_partner(side):
        return iy + (1 if side else -1)

    def row_ok(dx):
        return (ix + dx >= 0) & (ix + dx < X)

    barrier = pltpu.get_barrier_semaphore()
    for m in range(1, X):
        pl.semaphore_signal(barrier, inc=1, device_id=dev(lax.rem(ix + m, X), iy), device_id_type=MESH)
    near = jnp.int32(X - 1)
    for side in (0, 1):
        for dx in (-1, 0, 1):
            there = has_col[side] & row_ok(dx)
            near = near + there.astype(jnp.int32)

            @pl.when(there)
            def _():
                pl.semaphore_signal(
                    barrier, inc=1, device_id=dev(ix + dx, col_partner(side)), device_id_type=MESH
                )

    lane = lanes((LEV, T))
    edge[...] = jnp.zeros_like(edge)

    def pack_nest(n, carry):
        spot = (lane >= H * n) & (lane < H * n + H)
        k, r = n // N, lax.rem(n, N)
        left = nest[k, r, :, 0:T]
        right = nest[k, r, :, C - T : C]
        edge[0] = jnp.where(spot, pltpu.roll(left, H * n, 1), edge[0])
        edge[1] = jnp.where(spot, pltpu.roll(right, lax.rem(H * n + H, T), 1), edge[1])
        return carry

    def pack_parent(n, carry):
        spot = (lane >= 64 + H * n) & (lane < 64 + H * n + H)
        v = parent[n // R, lax.rem(n, R)]
        edge[0] = jnp.where(spot, pltpu.roll(v, 64 + H * n, 1), edge[0])
        edge[1] = jnp.where(spot, pltpu.roll(v, 64 + H * n + H, 1), edge[1])
        return carry

    lax.fori_loop(0, 3 * N, pack_nest, 0)
    lax.fori_loop(0, 3 * R, pack_parent, 0)

    pl.semaphore_wait(barrier, near)

    def pack_copy(side, dx):
        return rcopy(
            edge.at[side], pb.at[1 - dx, 1 - side], pack_ss.at[dx + 1, side], pack_rs.at[1 - dx, 1 - side],
            ix + dx, col_partner(side),
        )

    def ph_copy(down):
        if down:
            return rcopy(parent.at[:, 0], phb.at[1], ph_ss.at[1], ph_rs.at[1], ix - 1, iy)
        return rcopy(parent.at[:, R - 1], phb.at[0], ph_ss.at[0], ph_rs.at[0], ix + 1, iy)

    def halo_copy(down):
        if down:
            return rcopy(nest.at[:, 0:H], hh, halo_ss.at[1], halo_rs.at[1], ix - 1, iy)
        return rcopy(nest.at[:, N - H : N], hl, halo_ss.at[0], halo_rs.at[0], ix + 1, iy)

    for dx in (0, -1, 1):
        for side in (0, 1):
            there = has_col[side] & row_ok(dx)
            pl.when(there)(lambda: pack_copy(side, dx).start())
            pl.when(jnp.logical_not(there))(
                lambda: pb.__setitem__((dx + 1, side), jnp.zeros((LEV, T), F32))
            )
    pl.when(ix > 0)(lambda: ph_copy(True).start())
    pl.when(ix < X - 1)(lambda: ph_copy(False).start())
    early_down = (ix == 1) | (ix > half + 1)
    pl.when(early_down)(lambda: halo_copy(True).start())
    pl.when(ix < X - 1)(lambda: halo_copy(False).start())

    def pack_wait(dx):
        for side in (0, 1):
            pl.when(has_col[side] & row_ok(dx))(
                lambda: arrived(pb.at[dx + 1, side], pack_rs.at[dx + 1, side])
            )

    pack_wait(0)

    rim_spot = (lane < H) | (lane >= T - H)

    def unpack(dx, off):
        left = pltpu.roll(pb[dx + 1, 0], lax.rem(2 * T - H - off, T), 1)
        right = pltpu.roll(pb[dx + 1, 1], lax.rem(T - off, T), 1)
        return jnp.where(rim_spot, jnp.where(lane < T // 2, right, left), 0.0)

    def take_parent(n, carry):
        k, r = n // R, lax.rem(n, R)
        px[k, r + 1, :, 0:T] = parent[k, r]
        px[k, r + 1, :, T : 2 * T] = unpack(0, 64 + H * n)
        return carry

    lax.fori_loop(0, 3 * R, take_parent, 0)

    a0 = jnp.full((LEV, T), anchor[0], jnp.int32)
    first = (a0 - 1, a0 + (R * X // 2 - 4 - 1))

    def share(which):
        base = 1 if which else 0
        rims = 0 if which else 18

        def one(n, acc):
            t, k = n // 3, lax.rem(n, 3)
            body = jnp.zeros((LEV, T), F32)
            rim = jnp.zeros((LEV, T), F32)
            for i in range(R):
                hit = first[which] + t == R * ix + i
                body = jnp.where(hit, px[k, i + 1, :, 0:T], body)
                rim = jnp.where(hit, px[k, i + 1, :, T : 2 * T], rim)
            send_w[which, base + n] = body
            spot = (lane >= 6 * n) & (lane < 6 * n + 6)
            return jnp.where(spot, pltpu.roll(rim, lax.rem(6 * n + H, T), 1), acc)

        send_w[which, rims] = lax.fori_loop(0, 18, one, jnp.zeros((LEV, T), F32))

    in_west = ix <= half + 1
    in_east = ix >= half - 1
    pl.when(in_west)(lambda: share(WEST))
    pl.when(in_east)(lambda: share(EAST))

    def window_copy(which, part, x):
        span = (pl.ds(0, 4) if which else pl.ds(15, 4)) if part else pl.ds(0, 19)
        return rcopy(
            send_w.at[which, span], recv_w.at[which, span], win_ss.at[which], win_rs.at[which], x, iy
        )

    def window_pass(which, part, x, receives):
        if receives:
            span = (0, 4) if which and part else (15, 19) if part else (0, 19)
            window_copy(which, part, lax.rem(ix + 1, X)).wait_recv()

            def add(n, carry):
                send_w[which, n] = send_w[which, n] + recv_w[which, n]
                return carry

            lax.fori_loop(span[0], span[1], add, 0)

    pl.when(ix == half + 1)(lambda: window_copy(WEST, True, ix - 1).start())
    pl.when(ix == half - 1)(lambda: window_copy(EAST, True, ix + 1).start())
    late_down = (ix == half + 1) & (ix != 1)
    pl.when(late_down)(lambda: halo_copy(True).start())

    def take_rows(src, dx, first_row, count, at):
        def one(n, carry):
            k, r = n // count, lax.rem(n, count)
            sa[k, at + r, :, 0:C] = src[k, r]
            sa[k, at + r, :, C:W] = unpack(dx, H * (k * N + first_row + r))
            return carry

        lax.fori_loop(0, 3 * count, one, 0)

    take_rows(nest, 0, 0, N, H)

    @pl.when(ix == half)
    def _():
        window_pass(WEST, True, None, True)
        pl.when(ix > 0)(lambda: window_copy(WEST, False, ix - 1).start())
        pl.when(ix > 1)(lambda: halo_copy(True).start())
        window_pass(EAST, True, None, True)
        pl.when(ix < X - 1)(lambda: window_copy(EAST, False, ix + 1).start())

    if half > 1:

        @pl.when((ix > 0) & (ix < half))
        def _():
            window_pass(WEST, False, None, True)
            window_copy(WEST, False, ix - 1).start()
            pl.when(ix > 1)(lambda: halo_copy(True).start())

        @pl.when((ix > half) & (ix < X - 1))
        def _():
            window_pass(EAST, False, None, True)
            window_copy(EAST, False, ix + 1).start()

    cE, cW, cN, cS = range(4)

    def step(src, r, width):
        wide = width // T

        def cf(i):
            return jnp.concatenate([coef[i]] * wide, axis=1)

        def nb(k):
            x = src[k, r]
            return x, pltpu.roll(x, width - 1, 1), pltpu.roll(x, 1, 1)

        u, un, us = nb(0)
        v, vn, vs = nb(1)
        p, pn, ps = nb(2)

        def adv(k, x, xn, xs):
            return (
                0.5 * x + cf(cE) * src[k, r + 1] + cf(cW) * src[k, r - 1] + cf(cN) * xn + cf(cS) * xs
            )

        fu = adv(0, u, un, us) - 0.3 * (src[2, r + 1] - src[2, r - 1])
        fv = adv(1, v, vn, vs) - 0.3 * (pn - ps)
        fp = adv(2, p, pn, ps) - 0.3 * (src[0, r + 1] - src[0, r - 1] + (vn - vs))
        deep = mixer.shape[0]
        outs = []
        for f in (fu, fv, fp):
            full = f
            if deep > LEV:
                full = jnp.concatenate([f, jnp.zeros((deep - LEV, width), F32)], axis=0)
            hi, lo = split(full)
            stacked = jnp.concatenate([hi, hi, lo], axis=0)
            mixed = jnp.dot(mixer[...], stacked, preferred_element_type=F32)
            outs.append(f + mixed[:LEV])
        return outs

    @pl.when(ix > 0)
    def _():
        arrived(phb.at[0], ph_rs.at[0])

    @pl.when(ix < X - 1)
    def _():
        arrived(phb.at[1], ph_rs.at[1])

    pl.when(ix == 0)(lambda: phb.__setitem__(0, jnp.zeros((3, LEV, T), F32)))
    pl.when(ix == X - 1)(lambda: phb.__setitem__(1, jnp.zeros((3, LEV, T), F32)))
    for k in range(3):
        px[k, 0, :, 0:T] = phb[0, k]
        px[k, R + 1, :, 0:T] = phb[1, k]
        px[k, 0, :, T : 2 * T] = jnp.zeros((LEV, T), F32)
        px[k, R + 1, :, T : 2 * T] = jnp.zeros((LEV, T), F32)

    def parent_row(r, carry):
        for k, f in enumerate(step(px, r + 1, 2 * T)):
            parent_out[k, r] = f[:, 0:T]
        return carry

    lax.fori_loop(0, R, parent_row, 0)

    def masked(f, width):
        at = lanes((1, T))
        off_left = ((at >= T // 2) & (iy == 0)) | ((at < T // 2) & (iy == Y - 1))
        tail = jnp.where(off_left, 0.0, f[:, width - T : width])
        return jnp.concatenate([f[:, 0 : width - T], tail], axis=1)

    def run(src, dst, lo, hi):
        def one(r, carry):
            for k, f in enumerate(step(src, r, W)):
                dst[k, r] = masked(f, W)
            return carry

        lax.fori_loop(lo, hi, one, 0)

    def run_out(lo, hi):
        def one(r, carry):
            for k, f in enumerate(step(sb_last, r, W)):
                nest_out[k, r - H] = f[:, 0:C]
            return carry

        lax.fori_loop(lo, hi, one, 0)

    sb_last = sa
    top = N + 2 * H
    at_w, at_e = H + 3, H + N - 4
    lo1 = jnp.where(is_west, at_w + 1, 1)
    hi1 = jnp.where(is_east, at_e, top - 1)
    lo2 = jnp.where(is_west, at_w + 2, 2)
    hi2 = jnp.where(is_east, at_e - 1, top - 2)
    run(sa, sb, jnp.maximum(lo1, H + 1), jnp.minimum(hi1, H + N - 1))

    outer = is_west | is_east
    e = jnp.where(is_west, 0, 1)
    b_adj = jnp.where(is_west, 3, 0)

    def wt_copy(side):
        src = wx.at[:, :, C - T : C] if side else wx.at[:, :, 0:T]
        return rcopy(src, wrb.at[1 - side], wt_ss.at[side], wt_rs.at[1 - side], ix, col_partner(side))

    @pl.when(outer)
    def _():
        for row in range(4):
            for dc in range(3):
                acc = jnp.zeros((4, C), F32)
                for n in range(4):
                    hit = (d_rows[n, e] == row) & (d_cols[n, e] == dc - 1)
                    acc = acc + jnp.where(hit, d_wts[n, e], 0.0)
                wx[row * 3 + dc] = acc
        for side in (0, 1):
            pl.when(has_col[side])(lambda: wt_copy(side).start())
            pl.when(jnp.logical_not(has_col[side]))(
                lambda: wrb.__setitem__(side, jnp.zeros((12, 4, T), F32))
            )

    @pl.when(ix > 0)
    def _():
        pack_wait(-1)
        arrived(hl, halo_rs.at[0])
        take_rows(hl, -1, N - H, H, 0)

    @pl.when(ix < X - 1)
    def _():
        pack_wait(1)
        arrived(hh, halo_rs.at[1])
        take_rows(hh, 1, 0, H, H + N)

    run(sa, sb, lo1, jnp.minimum(hi1, H + 1))
    run(sa, sb, jnp.maximum(lo1, H + N - 1), hi1)
    run(sb, sa, lo2, hi2)

    def edge_work(which):
        base = 1 if which else 0
        rims = 0 if which else 18
        window_pass(which, False, None, True)

        def lay(n, carry):
            t, k = n // 3, lax.rem(n, 3)
            zb[k, t, :, 0:T] = send_w[which, base + n]
            tail = pltpu.roll(send_w[which, rims], lax.rem(2 * T - 6 * n - H, T), 1)
            zb[k, t, :, T : 2 * T] = jnp.where(rim_spot, tail, 0.0)
            return carry

        lax.fori_loop(0, 18, lay, 0)

    pl.when(is_west)(lambda: edge_work(WEST))
    pl.when(is_east)(lambda: edge_work(EAST))

    @pl.when(outer)
    def _():
        def zone_row(r, carry):
            for k, f in enumerate(step(zb, r + 1, 2 * T)):
                zn[k, r] = masked(f, 2 * T)
            return carry

        lax.fori_loop(0, 4, zone_row, 0)
        for side in (0, 1):
            pl.when(has_col[side])(lambda: arrived(wrb.at[side], wt_rs.at[side]))
        at8 = lanes((8, T))
        for b in range(4):
            for i in range(12):
                left = jnp.broadcast_to(wrb[0, i, b : b + 1, :], (8, T))
                right = jnp.broadcast_to(wrb[1, i, b : b + 1, :], (8, T))
                wxb[i, b, :, 0:C] = jnp.broadcast_to(wx[i, b : b + 1, :], (8, C))
                wxb[i, b, :, C:W] = jnp.where(at8 < T // 2, right, left)

        y = lanes((2 * T, W))
        c = lanes((2 * T, W), 0)
        y = jnp.where(y < C + T // 2, y, y - W)
        c = jnp.where(c < T + T // 2, c, c - 2 * T)
        for dc in range(3):
            gap = y - 3 * (c - (dc - 1))
            hot = jnp.where((gap >= 0) & (gap <= 2), 1.0, 0.0).astype(BF16)

            def spread(k, carry):
                for time in range(2):
                    rows = zn[k] if time else zb[k, 1:5]
                    hi, lo = split(rows.reshape(4 * LEV, 2 * T))
                    got = jnp.dot(hi, hot, preferred_element_type=F32) + jnp.dot(
                        lo, hot, preferred_element_type=F32
                    )
                    grid[time, k, dc] = got.reshape(4, LEV, W)
                return carry

            lax.fori_loop(0, 3, spread, 0)

        def bound(time, k, b):
            acc = jnp.zeros((LEV, W), F32)
            for row in range(4):
                for dc in range(3):
                    w = jnp.concatenate([wxb[row * 3 + dc, b]] * (LEV // 8), axis=0)
                    acc = acc + w * grid[time, k, dc, row]
            return acc

        def each(n, carry):
            k, b = n // 4, lax.rem(n, 4)
            got = bound(1, k, b)
            b1[b, k] = got
            nest_out[k, jnp.where(is_west, 0, N - 4) + b] = got[:, 0:C]
            return carry

        lax.fori_loop(0, 12, each, 0)

        def each0(k, carry):
            b0[k] = bound(0, k, b_adj)
            return carry

        lax.fori_loop(0, 3, each0, 0)

        ra = jnp.where(is_west, at_w, at_e)
        r2 = jnp.where(is_west, at_w + 1, at_e - 1)
        for k in range(3):
            sb[k, ra] = (1.0 - 1.0 / 3.0) * b0[k] + (1.0 / 3.0) * b1[b_adj, k]
        run(sb, sa, r2, r2 + 1)
        for k in range(3):
            sa[k, ra] = (1.0 - 2.0 / 3.0) * b0[k] + (2.0 / 3.0) * b1[b_adj, k]

    run_out(jnp.where(is_west, at_w + 1, H), jnp.where(is_east, at_e, H + N))

    per = N // 3
    sums = []
    for g in range(per):
        for k in range(3):
            sums.append(nest_out[k, 3 * g] + nest_out[k, 3 * g + 1] + nest_out[k, 3 * g + 2])
    hi, lo = split(jnp.concatenate(sums, axis=0))
    gap = lanes((C, T), 0) - 3 * lanes((C, T))
    pool = jnp.where((gap >= 0) & (gap <= 2), 1.0, 0.0).astype(BF16)
    mean = jnp.dot(hi, pool, preferred_element_type=F32) + jnp.dot(lo, pool, preferred_element_type=F32)
    co[...] = (mean * (1.0 / 9.0)).reshape(per, 3, LEV, T)

    def co_copy(g, m):
        return rcopy(co.at[g], cb.at[per * ix + g], co_ss.at[m, g], co_rs.at[per * ix + g], 1 + ix // 2 + m, iy)

    def co_each(action):
        for m in range(half):
            for g in range(per):
                inner = jnp.logical_not(is_west) if g == 0 else jnp.logical_not(is_east)
                pl.when(inner & (1 + ix // 2 + m != ix))(lambda: action(co_copy(g, m)))

    co_each(lambda copy: copy.start())

    def put(src, g):
        for i in range(R):
            hit = a0 + g == R * ix + i
            for k in range(3):
                parent_out[k, i] = jnp.where(hit, src[k], parent_out[k, i])

    def feed(g, carry):
        j = g // per
        reach = (1 + j // 2 <= ix) & (ix <= half + j // 2)

        @pl.when(reach & (j != ix))
        def _():
            arrived(cb.at[g], co_rs.at[g])
            put(cb.at[g], g)

        @pl.when(reach & (j == ix))
        def _():
            put(co.at[lax.rem(g, per)], g)

        return carry

    lax.fori_loop(1, per * X - 1, feed, 0)

    for dx in (0, -1, 1):
        for side in (0, 1):
            pl.when(has_col[side] & row_ok(dx))(lambda: pack_copy(side, dx).wait_send())
    pl.when(ix > 0)(lambda: ph_copy(True).wait_send())
    pl.when(ix < X - 1)(lambda: ph_copy(False).wait_send())
    pl.when(ix > 0)(lambda: halo_copy(True).wait_send())
    pl.when(ix < X - 1)(lambda: halo_copy(False).wait_send())
    pl.when(ix == half + 1)(lambda: window_copy(WEST, True, ix - 1).wait_send())
    pl.when((ix > 0) & (ix <= half))(lambda: window_copy(WEST, False, ix - 1).wait_send())
    pl.when(ix == half - 1)(lambda: window_copy(EAST, True, ix + 1).wait_send())
    pl.when((ix >= half) & (ix < X - 1))(lambda: window_copy(EAST, False, ix + 1).wait_send())
    for side in (0, 1):
        pl.when(outer & has_col[side])(lambda: wt_copy(side).wait_send())
    co_each(lambda copy: copy.wait_send())


def shards(parent, nest, nest_anchor, donor_rows, donor_cols, donor_weights, wind_x, wind_y, column_mix):
    X = lax.axis_size("gx")
    CY = lax.axis_size("gz")
    Y = lax.axis_size("gy") * CY
    LEV, R = parent.shape[1], parent.shape[2]
    N, C = nest.shape[2], nest.shape[3]
    W = C + T
    top = N + 2 * H
    per = N // 3
    deep = -(-LEV // 16) * 16
    hi = lax.reduce_precision(column_mix, 8, 7)
    hi, lo = (jnp.pad(x, ((0, deep - LEV), (0, deep - LEV))) for x in (hi, column_mix - hi))
    mixer = jnp.concatenate([hi, lo, hi], axis=1).astype(BF16)
    wx, wy = 0.5 * wind_x, 0.5 * wind_y
    coef = jnp.stack([0.125 - wx, 0.125 + wx, 0.125 - wy, 0.125 + wy])
    coef = jnp.broadcast_to(coef[:, :, None], (4, LEV, T))
    vmem = pl.BlockSpec(memory_space=pltpu.VMEM)
    smem = pl.BlockSpec(memory_space=pltpu.SMEM)
    V = lambda *s: pltpu.VMEM(s, F32)
    D = lambda *s: pltpu.SemaphoreType.DMA(s)
    outs = pl.pallas_call(
        functools.partial(kernel, X, Y, CY),
        out_shape=(
            jax.ShapeDtypeStruct((3, R, LEV, T), F32),
            jax.ShapeDtypeStruct((3, N, LEV, C), F32),
        ),
        in_specs=[vmem, vmem, smem, vmem, vmem, vmem, vmem, vmem],
        out_specs=(vmem, vmem),
        scratch_shapes=[
            V(2, LEV, T),
            V(3, 2, LEV, T),
            V(2, 3, LEV, T),
            V(3, H, LEV, C),
            V(3, H, LEV, C),
            V(3, R + 2, LEV, 2 * T),
            V(3, top, LEV, W),
            V(3, top, LEV, W),
            V(2, 19, LEV, T),
            V(2, 19, LEV, T),
            V(3, 6, LEV, 2 * T),
            V(3, 4, LEV, 2 * T),
            V(2, 3, 3, 4, LEV, W),
            V(12, 4, C),
            V(2, 12, 4, T),
            V(12, 4, 8, W),
            V(3, LEV, W),
            V(4, 3, LEV, W),
            V(per, 3, LEV, T),
            V(per * X, 3, LEV, T),
            D(3, 2), D(3, 2), D(2), D(2), D(2), D(2), D(2), D(2), D(2), D(2), D(X // 2, per), D(per * X),
        ],
        compiler_params=pltpu.CompilerParams(
            collective_id=0, has_side_effects=True, vmem_limit_bytes=48 * 1024 * 1024
        ),
        cost_estimate=pl.CostEstimate(flops=200_000_000, bytes_accessed=6_000_000, transcendentals=0),
    )(
        parent.transpose(0, 2, 1, 3),
        nest.transpose(0, 2, 1, 3),
        nest_anchor,
        donor_rows,
        donor_cols,
        donor_weights,
        coef,
        mixer,
    )
    return tuple(x.transpose(0, 2, 1, 3) for x in outs)


def solution(mesh):
    grids = P("member", None, "gx", ("gy", "gz"))
    donors = P("member", None, None, ("gy", "gz"))
    return jax.shard_map(
        shards,
        mesh=mesh,
        in_specs=(grids, grids, P("member"), donors, donors, donors, P(), P(), P()),
        out_specs=(grids, grids),
        check_vma=False,
    )
```

```python
import functools

import jax
import jax.numpy as jnp
from jax import lax
from jax.experimental import pallas as pl
from jax.experimental.pallas import tpu as pltpu
from jax.sharding import PartitionSpec as P

MESH = pl.DeviceIdType.MESH
F32 = jnp.float32
BF16 = jnp.bfloat16
T = 128
H = 3
WEST, EAST = 0, 1


def lanes(shape, dim=1):
    return lax.broadcasted_iota(jnp.int32, shape, dim)


def split(x):
    hi = x.astype(BF16)
    lo = (x - hi.astype(F32)).astype(BF16)
    return hi, lo


def kernel(
    X, Y, CY,
    parent_in, nest_in, anchor, rows_in, cols_in, wts_in, wind_x_in, wind_y_in, mix_in,
    parent_out, nest_out,
    raw, nest, d_rows, d_cols, d_wts, wind_x, wind_y, mix, parent, coef, mixer, packed, hot,
    edge, pb, phb, hl, hh, px, sa, sb, send_w, recv_w, zb, zn, grid, wx, wrb, wxb, b0, b1, co, cb, load_s,
    pack_ss, pack_rs, ph_ss, ph_rs, halo_ss, halo_rs, win_ss, win_rs, wt_ss, wt_rs, co_ss, co_rs,
):
    pairs = (
        (nest_in, nest), (parent_in, raw), (wind_x_in, wind_x), (wind_y_in, wind_y), (mix_in, mix),
        (rows_in, d_rows), (cols_in, d_cols), (wts_in, d_wts),
    )
    loads = [pltpu.make_async_copy(a, b, load_s.at[i]) for i, (a, b) in enumerate(pairs)]
    for load in loads:
        load.start()
    R = parent.shape[1]
    N = nest.shape[1]
    LEV = nest.shape[2]
    C = nest.shape[3]
    W = C + T
    me = lax.axis_index("member")
    ix = lax.axis_index("gx")
    iy = lax.axis_index("gy") * CY + lax.axis_index("gz")
    half = X // 2
    is_west = ix == 0
    is_east = ix == X - 1
    has_col = (iy > 0, iy < Y - 1)

    def dev(x, y):
        return (me, x, y // CY, lax.rem(y, CY))

    def rcopy(src, dst, ss, rs, x, y):
        return pltpu.make_async_remote_copy(
            src_ref=src, dst_ref=dst, send_sem=ss, recv_sem=rs, device_id=dev(x, y), device_id_type=MESH
        )

    def arrived(ref, rs):
        rcopy(ref, ref, halo_ss.at[0, 0], rs, lax.rem(ix + 1, X), iy).wait_recv()

    def col_partner(side):
        return iy + (1 if side else -1)

    def row_ok(dx):
        return (ix + dx >= 0) & (ix + dx < X)

    barrier = pltpu.get_barrier_semaphore()
    for m in range(1, X):
        pl.semaphore_signal(barrier, inc=1, device_id=dev(lax.rem(ix + m, X), iy), device_id_type=MESH)
    near = jnp.int32(X - 1)
    for side in (0, 1):
        for dx in (-1, 0, 1):
            there = has_col[side] & row_ok(dx)
            near = near + there.astype(jnp.int32)

            @pl.when(there)
            def _():
                pl.semaphore_signal(
                    barrier, inc=1, device_id=dev(ix + dx, col_partner(side)), device_id_type=MESH
                )

    lane = lanes((LEV, T))
    loads[0].wait()
    loads[1].wait()
    for k in range(3):
        for r in range(R):
            parent[k, r] = raw[k, :, r, :]
    edge[...] = jnp.zeros_like(edge)

    def pack_nest(n, carry):
        spot = (lane >= H * n) & (lane < H * n + H)
        k, r = n // N, lax.rem(n, N)
        left = nest[k, r, :, 0:T]
        right = nest[k, r, :, C - T : C]
        edge[0] = jnp.where(spot, pltpu.roll(left, H * n, 1), edge[0])
        edge[1] = jnp.where(spot, pltpu.roll(right, lax.rem(H * n + H, T), 1), edge[1])
        return carry

    def pack_parent(n, carry):
        spot = (lane >= 64 + H * n) & (lane < 64 + H * n + H)
        v = parent[n // R, lax.rem(n, R)]
        edge[0] = jnp.where(spot, pltpu.roll(v, 64 + H * n, 1), edge[0])
        edge[1] = jnp.where(spot, pltpu.roll(v, 64 + H * n + H, 1), edge[1])
        return carry

    lax.fori_loop(0, 3 * N, pack_nest, 0)
    lax.fori_loop(0, 3 * R, pack_parent, 0)

    pl.semaphore_wait(barrier, near)

    def pack_copy(side, dx):
        return rcopy(
            edge.at[side], pb.at[1 - dx, 1 - side], pack_ss.at[dx + 1, side], pack_rs.at[1 - dx, 1 - side],
            ix + dx, col_partner(side),
        )

    def ph_copy(down):
        if down:
            return rcopy(parent.at[:, 0], phb.at[1], ph_ss.at[1], ph_rs.at[1], ix - 1, iy)
        return rcopy(parent.at[:, R - 1], phb.at[0], ph_ss.at[0], ph_rs.at[0], ix + 1, iy)

    def halo_copy(down, j):
        if down:
            return rcopy(nest.at[:, j], hh.at[:, j], halo_ss.at[1, j], halo_rs.at[1, j], ix - 1, iy)
        i = H - 1 - j
        return rcopy(nest.at[:, N - 1 - j], hl.at[:, i], halo_ss.at[0, j], halo_rs.at[0, j], ix + 1, iy)

    def halo_send(down, rows):
        for j in rows:
            halo_copy(down, j).start()

    for dx in (0, -1, 1):
        for side in (0, 1):
            there = has_col[side] & row_ok(dx)
            pl.when(there)(lambda: pack_copy(side, dx).start())
            pl.when(jnp.logical_not(there))(
                lambda: pb.__setitem__((dx + 1, side), jnp.zeros((LEV, T), F32))
            )
    pl.when(ix > 0)(lambda: ph_copy(True).start())
    pl.when(ix < X - 1)(lambda: ph_copy(False).start())
    pl.when(ix > 0)(lambda: halo_send(True, (0,)))
    pl.when(ix < X - 1)(lambda: halo_send(False, (0,)))
    pl.when(ix > half)(lambda: halo_send(True, (1, 2)))
    pl.when(ix < half)(lambda: halo_send(False, (1, 2)))

    def pack_wait(dx):
        for side in (0, 1):
            pl.when(has_col[side] & row_ok(dx))(
                lambda: arrived(pb.at[dx + 1, side], pack_rs.at[dx + 1, side])
            )

    pack_wait(0)

    rim_spot = (lane < H) | (lane >= T - H)

    def unpack(dx, off):
        left = pltpu.roll(pb[dx + 1, 0], lax.rem(2 * T - H - off, T), 1)
        right = pltpu.roll(pb[dx + 1, 1], lax.rem(T - off, T), 1)
        return jnp.where(rim_spot, jnp.where(lane < T // 2, right, left), 0.0)

    def take_parent(n, carry):
        k, r = n // R, lax.rem(n, R)
        px[k, r + 1, :, 0:T] = parent[k, r]
        px[k, r + 1, :, T : 2 * T] = unpack(0, 64 + H * n)
        return carry

    lax.fori_loop(0, 3 * R, take_parent, 0)

    a0 = jnp.full((LEV, T), anchor[0], jnp.int32)
    first = (a0 - 1, a0 + (R * X // 2 - 4 - 1))

    def share(which):
        base = 1 if which else 0
        rims = 0 if which else 18

        def one(n, acc):
            t, k = n // 3, lax.rem(n, 3)
            body = jnp.zeros((LEV, T), F32)
            rim = jnp.zeros((LEV, T), F32)
            for i in range(R):
                hit = first[which] + t == R * ix + i
                body = jnp.where(hit, px[k, i + 1, :, 0:T], body)
                rim = jnp.where(hit, px[k, i + 1, :, T : 2 * T], rim)
            send_w[which, base + n] = body
            spot = (lane >= 6 * n) & (lane < 6 * n + 6)
            return jnp.where(spot, pltpu.roll(rim, lax.rem(6 * n + H, T), 1), acc)

        send_w[which, rims] = lax.fori_loop(0, 18, one, jnp.zeros((LEV, T), F32))

    in_west = ix <= half + 1
    in_east = ix >= half - 1
    pl.when(in_west)(lambda: share(WEST))
    pl.when(in_east)(lambda: share(EAST))

    spans = (((0, 6), (6, 12), (12, 15), (15, 19)), ((13, 19), (7, 13), (4, 7), (0, 4)))

    def window_copy(which, c, x):
        lo, hi = spans[which][c]
        span = pl.ds(lo, hi - lo)
        return rcopy(
            send_w.at[which, span], recv_w.at[which, span], win_ss.at[which, c], win_rs.at[which, c], x, iy
        )

    def window_add(which, c):
        window_copy(which, c, lax.rem(ix + 1, X)).wait_recv()

        def add(n, carry):
            send_w[which, n] = send_w[which, n] + recv_w[which, n]
            return carry

        lax.fori_loop(spans[which][c][0], spans[which][c][1], add, 0)

    pl.when(ix == half + 1)(lambda: window_copy(WEST, 3, ix - 1).start())
    pl.when(ix == half - 1)(lambda: window_copy(EAST, 3, ix + 1).start())

    @pl.when(ix == half)
    def _():
        for c in range(3):
            window_copy(WEST, c, ix - 1).start()
            if half < X - 1:
                window_copy(EAST, c, ix + 1).start()

    def take_rows(src, dx, first_row, count, at, only=None):
        def one(n, carry):
            k, r = (n // count, n % count) if only is not None else (n // count, lax.rem(n, count))
            sa[k, at + r, :, 0:C] = src[k, r]
            sa[k, at + r, :, C:W] = unpack(dx, H * (k * N + first_row + r))
            return carry

        if only is None:
            lax.fori_loop(0, 3 * count, one, 0)
        else:
            for k in range(3):
                one(k * count + only, 0)

    take_rows(nest, 0, 0, N, H)

    @pl.when(ix == half)
    def _():
        window_add(WEST, 3)
        window_copy(WEST, 3, ix - 1).start()
        window_add(EAST, 3)
        if half < X - 1:
            window_copy(EAST, 3, ix + 1).start()

    if half > 1:

        @pl.when((ix > 0) & (ix < half))
        def _():
            for c in range(4):
                window_add(WEST, c)
                window_copy(WEST, c, ix - 1).start()

    if half + 1 < X - 1:

        @pl.when((ix > half) & (ix < X - 1))
        def _():
            for c in range(4):
                window_add(EAST, c)
                window_copy(EAST, c, ix + 1).start()

    pl.when((ix > 0) & (ix <= half))(lambda: halo_send(True, (1, 2)))
    pl.when((ix < X - 1) & (ix >= half))(lambda: halo_send(False, (1, 2)))

    for load in loads[2:5]:
        load.wait()
    diagonal = lanes((LEV, LEV)) == lanes((LEV, LEV), 0)

    def column(ref):
        w = jnp.where(diagonal, jnp.broadcast_to(ref[...], (LEV, LEV)), 0.0)
        return jnp.broadcast_to(0.5 * jnp.sum(w, axis=1, keepdims=True), (LEV, T))

    wind = column(wind_x)
    coef[0] = 0.125 - wind
    coef[1] = 0.125 + wind
    wind = column(wind_y)
    coef[2] = 0.125 - wind
    coef[3] = 0.125 + wind
    mixer[...] = jnp.zeros_like(mixer)
    for i in range(3):
        whole = mix[...]
        top_part = whole.astype(BF16).astype(F32)
        mixer[i, 0:LEV, 0:LEV] = whole - top_part if i == 1 else top_part
    DEEP = mixer.shape[2]
    placed = mixer[0] + pltpu.roll(mixer[1], LEV, 1) + pltpu.roll(mixer[2], 2 * LEV, 1)
    packed[...] = placed.astype(BF16)
    cE, cW, cN, cS = range(4)

    def step(src, r, width):
        wide = width // T

        def cf(i):
            return jnp.concatenate([coef[i]] * wide, axis=1)

        def nb(k):
            x = src[k, r]
            return x, pltpu.roll(x, width - 1, 1), pltpu.roll(x, 1, 1)

        u, un, us = nb(0)
        v, vn, vs = nb(1)
        p, pn, ps = nb(2)

        def adv(k, x, xn, xs):
            return (
                0.5 * x + cf(cE) * src[k, r + 1] + cf(cW) * src[k, r - 1] + cf(cN) * xn + cf(cS) * xs
            )

        fu = adv(0, u, un, us) - 0.3 * (src[2, r + 1] - src[2, r - 1])
        fv = adv(1, v, vn, vs) - 0.3 * (pn - ps)
        fp = adv(2, p, pn, ps) - 0.3 * (src[0, r + 1] - src[0, r - 1] + (vn - vs))
        outs = []
        for f in (fu, fv, fp):
            hi = f.astype(BF16).astype(F32)
            stacked = jnp.concatenate([hi, hi, f - hi], axis=0)
            if DEEP > 3 * LEV:
                stacked = jnp.concatenate([stacked, jnp.zeros((DEEP - 3 * LEV, width), F32)], axis=0)
            mixed = jnp.dot(packed[...], stacked.astype(BF16), preferred_element_type=F32)
            outs.append(f + mixed[:LEV])
        return outs

    @pl.when(ix > 0)
    def _():
        arrived(phb.at[0], ph_rs.at[0])

    @pl.when(ix < X - 1)
    def _():
        arrived(phb.at[1], ph_rs.at[1])

    pl.when(ix == 0)(lambda: phb.__setitem__(0, jnp.zeros((3, LEV, T), F32)))
    pl.when(ix == X - 1)(lambda: phb.__setitem__(1, jnp.zeros((3, LEV, T), F32)))
    for k in range(3):
        px[k, 0, :, 0:T] = phb[0, k]
        px[k, R + 1, :, 0:T] = phb[1, k]
        px[k, 0, :, T : 2 * T] = jnp.zeros((LEV, T), F32)
        px[k, R + 1, :, T : 2 * T] = jnp.zeros((LEV, T), F32)

    def parent_row(r, carry):
        for k, f in enumerate(step(px, r + 1, 2 * T)):
            parent_out[k, r] = f[:, 0:T]
        return carry

    lax.fori_loop(0, R, parent_row, 0)

    def masked(f, width):
        at = lanes((1, T))
        off_left = ((at >= T // 2) & (iy == 0)) | ((at < T // 2) & (iy == Y - 1))
        tail = jnp.where(off_left, 0.0, f[:, width - T : width])
        return jnp.concatenate([f[:, 0 : width - T], tail], axis=1)

    def run(src, dst, lo, hi):
        def one(r, carry):
            for k, f in enumerate(step(src, r, W)):
                dst[k, r] = masked(f, W)
            return carry

        lax.fori_loop(lo, hi, one, 0)

    def run_out(r):
        for k, f in enumerate(step(sa, r, W)):
            nest_out[k, r - H] = f[:, 0:C]

    top = N + 2 * H
    at_w, at_e = H + 3, H + N - 4
    outer = is_west | is_east
    inner = jnp.logical_not(outer)
    run(sa, sb, jnp.where(is_west, at_w + 1, H + 1), jnp.where(is_east, at_e, H + N - 1))

    @pl.when(inner)
    def _():
        run(sb, sa, H + 2, H + N - 2)

    e = jnp.where(is_west, 0, 1)
    b_adj = jnp.where(is_west, 3, 0)

    def wt_copy(side):
        src = wx.at[:, :, C - T : C] if side else wx.at[:, :, 0:T]
        return rcopy(src, wrb.at[1 - side], wt_ss.at[side], wt_rs.at[1 - side], ix, col_partner(side))

    for load in loads[5:]:
        load.wait()

    @pl.when(outer)
    def _():
        for row in range(4):
            for dc in range(3):
                acc = jnp.zeros((4, C), F32)
                for n in range(4):
                    hit = (d_rows[n, e] == row) & (d_cols[n, e] == dc - 1)
                    acc = acc + jnp.where(hit, d_wts[n, e], 0.0)
                wx[row * 3 + dc] = acc
        for side in (0, 1):
            pl.when(has_col[side])(lambda: wt_copy(side).start())
            pl.when(jnp.logical_not(has_col[side]))(
                lambda: wrb.__setitem__(side, jnp.zeros((12, 4, T), F32))
            )

    def take(j, low):
        if low:
            arrived(hl.at[:, H - 1 - j], halo_rs.at[0, j])
            take_rows(hl, -1, N - H, H, 0, H - 1 - j)
        else:
            arrived(hh.at[:, j], halo_rs.at[1, j])
            take_rows(hh, 1, 0, H, H + N, j)

    def at(j, s, low):
        return H - j + s - 1 if low else H + N - 1 + j - s + 1

    def one_row(src, dst, r):
        run(src, dst, r, r + 1)

    def grow(j, low):
        one_row(sa, sb, at(j, 1, low))
        one_row(sb, sa, at(j, 2, low))
        run_out(at(j, 3, low))

    @pl.when(ix > 0)
    def _():
        pack_wait(-1)
        take(0, True)
        one_row(sa, sb, at(0, 1, True))

    @pl.when(ix < X - 1)
    def _():
        pack_wait(1)
        take(0, False)
        one_row(sa, sb, at(0, 1, False))

    @pl.when(outer)
    def _():
        for side in (0, 1):
            pl.when(has_col[side])(lambda: arrived(wrb.at[side], wt_rs.at[side]))
        at8 = lanes((8, T))
        for b in range(4):
            for i in range(12):
                left = jnp.broadcast_to(wrb[0, i, b : b + 1, :], (8, T))
                right = jnp.broadcast_to(wrb[1, i, b : b + 1, :], (8, T))
                wxb[i, b, :, 0:C] = jnp.broadcast_to(wx[i, b : b + 1, :], (8, C))
                wxb[i, b, :, C:W] = jnp.where(at8 < T // 2, right, left)

        y = lanes((2 * T, W))
        c = lanes((2 * T, W), 0)
        y = jnp.where(y < C + T // 2, y, y - W)
        c = jnp.where(c < T + T // 2, c, c - 2 * T)
        for dc in range(3):
            gap = y - 3 * (c - (dc - 1))
            hot[dc] = jnp.where((gap >= 0) & (gap <= 2), 1.0, 0.0).astype(BF16)

    def edge_work(which):
        base = 1 if which else 0
        rims = 0 if which else 18
        for c in range(4):
            window_add(which, c)

        def lay(n, carry):
            t, k = n // 3, lax.rem(n, 3)
            zb[k, t, :, 0:T] = send_w[which, base + n]
            tail = pltpu.roll(send_w[which, rims], lax.rem(2 * T - 6 * n - H, T), 1)
            zb[k, t, :, T : 2 * T] = jnp.where(rim_spot, tail, 0.0)
            return carry

        lax.fori_loop(0, 18, lay, 0)

    pl.when(is_west)(lambda: edge_work(WEST))
    pl.when(is_east)(lambda: edge_work(EAST))

    @pl.when(outer)
    def _():
        def zone_row(r, carry):
            for k, f in enumerate(step(zb, r + 1, 2 * T)):
                zn[k, r] = masked(f, 2 * T)
            return carry

        lax.fori_loop(0, 4, zone_row, 0)
        for dc in range(3):

            def spread(k, carry):
                for time in range(2):
                    rows = zn[k] if time else zb[k, 1:5]
                    hi, lo = split(rows.reshape(4 * LEV, 2 * T))
                    got = jnp.dot(hi, hot[dc], preferred_element_type=F32) + jnp.dot(
                        lo, hot[dc], preferred_element_type=F32
                    )
                    grid[time, k, dc] = got.reshape(4, LEV, W)
                return carry

            lax.fori_loop(0, 3, spread, 0)

        def bound(time, k, b):
            acc = jnp.zeros((LEV, W), F32)
            for row in range(4):
                for dc in range(3):
                    w = jnp.concatenate([wxb[row * 3 + dc, b]] * (LEV // 8), axis=0)
                    acc = acc + w * grid[time, k, dc, row]
            return acc

        def each(n, carry):
            k, b = n // 4, lax.rem(n, 4)
            got = bound(1, k, b)
            b1[b, k] = got
            nest_out[k, jnp.where(is_west, 0, N - 4) + b] = got[:, 0:C]
            return carry

        lax.fori_loop(0, 12, each, 0)

        def each0(k, carry):
            b0[k] = bound(0, k, b_adj)
            return carry

        lax.fori_loop(0, 3, each0, 0)

        ra = jnp.where(is_west, at_w, at_e)
        for k in range(3):
            sb[k, ra] = (1.0 - 1.0 / 3.0) * b0[k] + (1.0 / 3.0) * b1[b_adj, k]
            sa[k, ra] = (1.0 - 2.0 / 3.0) * b0[k] + (2.0 / 3.0) * b1[b_adj, k]

    @pl.when(ix > 0)
    def _():
        one_row(sb, sa, at(0, 2, True))
        pl.when(inner)(lambda: run_out(at(0, 3, True)))

    @pl.when(ix < X - 1)
    def _():
        one_row(sb, sa, at(0, 2, False))
        pl.when(inner)(lambda: run_out(at(0, 3, False)))

    for low in (True, False):

        @pl.when(ix > 0 if low else ix < X - 1)
        def _():
            for j in (1, 2):
                take(j, low)
                grow(j, low)

    per = N // 3
    sums = []
    for g in range(per):
        for k in range(3):
            sums.append(nest_out[k, 3 * g] + nest_out[k, 3 * g + 1] + nest_out[k, 3 * g + 2])
    hi, lo = split(jnp.concatenate(sums, axis=0))
    gap = lanes((C, T), 0) - 3 * lanes((C, T))
    pool = jnp.where((gap >= 0) & (gap <= 2), 1.0, 0.0).astype(BF16)
    mean = jnp.dot(hi, pool, preferred_element_type=F32) + jnp.dot(lo, pool, preferred_element_type=F32)
    co[...] = (mean * (1.0 / 9.0)).reshape(per, 3, LEV, T)

    def co_copy(g, m):
        return rcopy(co.at[g], cb.at[per * ix + g], co_ss.at[m, g], co_rs.at[per * ix + g], 1 + ix // 2 + m, iy)

    def co_each(action):
        for m in range(half):
            for g in range(per):
                inner = jnp.logical_not(is_west) if g == 0 else jnp.logical_not(is_east)
                pl.when(inner & (1 + ix // 2 + m != ix))(lambda: action(co_copy(g, m)))

    co_each(lambda copy: copy.start())

    def put(src, g):
        for i in range(R):
            hit = a0 + g == R * ix + i
            for k in range(3):
                parent_out[k, i] = jnp.where(hit, src[k], parent_out[k, i])

    def feed(g, carry):
        j = g // per
        reach = (1 + j // 2 <= ix) & (ix <= half + j // 2)

        @pl.when(reach & (j != ix))
        def _():
            arrived(cb.at[g], co_rs.at[g])
            put(cb.at[g], g)

        @pl.when(reach & (j == ix))
        def _():
            put(co.at[lax.rem(g, per)], g)

        return carry

    lax.fori_loop(1, per * X - 1, feed, 0)

    for dx in (0, -1, 1):
        for side in (0, 1):
            pl.when(has_col[side] & row_ok(dx))(lambda: pack_copy(side, dx).wait_send())
    pl.when(ix > 0)(lambda: ph_copy(True).wait_send())
    pl.when(ix < X - 1)(lambda: ph_copy(False).wait_send())
    for j in range(H):
        pl.when(ix > 0)(lambda: halo_copy(True, j).wait_send())
        pl.when(ix < X - 1)(lambda: halo_copy(False, j).wait_send())
    pl.when(ix == half + 1)(lambda: window_copy(WEST, 3, ix - 1).wait_send())
    pl.when(ix == half - 1)(lambda: window_copy(EAST, 3, ix + 1).wait_send())
    for c in range(4):
        pl.when((ix > 0) & (ix <= half))(lambda: window_copy(WEST, c, ix - 1).wait_send())
        pl.when((ix >= half) & (ix < X - 1))(lambda: window_copy(EAST, c, ix + 1).wait_send())
    for side in (0, 1):
        pl.when(outer & has_col[side])(lambda: wt_copy(side).wait_send())
    co_each(lambda copy: copy.wait_send())


def shards(parent, nest, nest_anchor, donor_rows, donor_cols, donor_weights, wind_x, wind_y, column_mix):
    X = lax.axis_size("gx")
    CY = lax.axis_size("gz")
    Y = lax.axis_size("gy") * CY
    LEV, R = parent.shape[1], parent.shape[2]
    N, C = nest.shape[2], nest.shape[3]
    W = C + T
    top = N + 2 * H
    per = N // 3
    deep = -(-3 * LEV // T) * T
    LEVP = -(-LEV // 16) * 16
    vmem = pl.BlockSpec(memory_space=pltpu.VMEM)
    hbm = pl.BlockSpec(memory_space=pltpu.HBM)
    smem = pl.BlockSpec(memory_space=pltpu.SMEM)
    V = lambda *s: pltpu.VMEM(s, F32)
    I = lambda *s: pltpu.VMEM(s, jnp.int32)
    D = lambda *s: pltpu.SemaphoreType.DMA(s)
    outs = pl.pallas_call(
        functools.partial(kernel, X, Y, CY),
        out_shape=(
            jax.ShapeDtypeStruct((3, R, LEV, T), F32),
            jax.ShapeDtypeStruct((3, N, LEV, C), F32),
        ),
        in_specs=[hbm, hbm, smem, hbm, hbm, hbm, hbm, hbm, hbm],
        out_specs=(vmem, vmem),
        scratch_shapes=[
            V(3, LEV, R, T),
            V(3, N, LEV, C),
            I(4, 2, 4, C),
            I(4, 2, 4, C),
            V(4, 2, 4, C),
            V(1, LEV),
            V(1, LEV),
            V(LEV, LEV),
            V(3, R, LEV, T),
            V(4, LEV, T),
            V(3, LEVP, deep),
            pltpu.VMEM((LEVP, deep), BF16),
            pltpu.VMEM((3, 2 * T, W), BF16),
            V(2, LEV, T),
            V(3, 2, LEV, T),
            V(2, 3, LEV, T),
            V(3, H, LEV, C),
            V(3, H, LEV, C),
            V(3, R + 2, LEV, 2 * T),
            V(3, top, LEV, W),
            V(3, top, LEV, W),
            V(2, 19, LEV, T),
            V(2, 19, LEV, T),
            V(3, 6, LEV, 2 * T),
            V(3, 4, LEV, 2 * T),
            V(2, 3, 3, 4, LEV, W),
            V(12, 4, C),
            V(2, 12, 4, T),
            V(12, 4, 8, W),
            V(3, LEV, W),
            V(4, 3, LEV, W),
            V(per, 3, LEV, T),
            V(per * X, 3, LEV, T),
            D(8),
            D(3, 2), D(3, 2), D(2), D(2), D(2, H), D(2, H), D(2, 4), D(2, 4), D(2), D(2), D(X // 2, per), D(per * X),
        ],
        compiler_params=pltpu.CompilerParams(
            collective_id=0, has_side_effects=True, vmem_limit_bytes=48 * 1024 * 1024
        ),
        cost_estimate=pl.CostEstimate(flops=200_000_000, bytes_accessed=6_000_000, transcendentals=0),
    )(
        parent,
        nest.transpose(0, 2, 1, 3),
        nest_anchor,
        donor_rows,
        donor_cols,
        donor_weights,
        wind_x.reshape(1, LEV),
        wind_y.reshape(1, LEV),
        column_mix,
    )
    return tuple(x.transpose(0, 2, 1, 3) for x in outs)


def solution(mesh):
    grids = P("member", None, "gx", ("gy", "gz"))
    donors = P("member", None, None, ("gy", "gz"))
    return jax.shard_map(
        shards,
        mesh=mesh,
        in_specs=(grids, grids, P("member"), donors, donors, donors, P(), P(), P()),
        out_specs=(grids, grids),
        check_vma=False,
    )
```

```python
import functools

import jax
import jax.numpy as jnp
from jax import lax
from jax.experimental import pallas as pl
from jax.experimental.pallas import tpu as pltpu
from jax.sharding import PartitionSpec as P

MESH = pl.DeviceIdType.MESH
F32 = jnp.float32
BF16 = jnp.bfloat16
T = 128
H = 3
WEST, EAST = 0, 1


def lanes(shape, dim=1):
    return lax.broadcasted_iota(jnp.int32, shape, dim)


def split(x):
    hi = x.astype(BF16)
    lo = (x - hi.astype(F32)).astype(BF16)
    return hi, lo


def kernel(
    X, Y, CY,
    parent_in, nest_in, anchor, rows_in, cols_in, wts_in, wind_x_in, wind_y_in, mix_in,
    parent_out, nest_out,
    raw, nest, d_rows, d_cols, d_wts, wind_x, wind_y, mix, parent, coef, mixer, packed, hot,
    edge, pb, phb, hl, hh, px, sa, sb, send_w, recv_w, zb, zn, grid, wx, wrb, wxb, b0, b1, co, cb, load_s,
    pack_ss, pack_rs, ph_ss, ph_rs, halo_ss, halo_rs, win_ss, win_rs, wt_ss, wt_rs, co_ss, co_rs,
):
    pairs = (
        (nest_in, nest), (parent_in, raw), (wind_x_in, wind_x), (wind_y_in, wind_y), (mix_in, mix),
        (rows_in, d_rows), (cols_in, d_cols), (wts_in, d_wts),
    )
    loads = [pltpu.make_async_copy(a, b, load_s.at[i]) for i, (a, b) in enumerate(pairs)]
    for load in loads:
        load.start()
    R = parent.shape[1]
    N = nest.shape[1]
    LEV = nest.shape[2]
    C = nest.shape[3]
    W = C + T
    me = lax.axis_index("member")
    ix = lax.axis_index("gx")
    iy = lax.axis_index("gy") * CY + lax.axis_index("gz")
    half = X // 2
    is_west = ix == 0
    is_east = ix == X - 1
    has_col = (iy > 0, iy < Y - 1)

    def dev(x, y):
        return (me, x, y // CY, lax.rem(y, CY))

    def rcopy(src, dst, ss, rs, x, y):
        return pltpu.make_async_remote_copy(
            src_ref=src, dst_ref=dst, send_sem=ss, recv_sem=rs, device_id=dev(x, y), device_id_type=MESH
        )

    def arrived(ref, rs):
        rcopy(ref, ref, halo_ss.at[0, 0], rs, lax.rem(ix + 1, X), iy).wait_recv()

    def col_partner(side):
        return iy + (1 if side else -1)

    def row_ok(dx):
        return (ix + dx >= 0) & (ix + dx < X)

    barrier = pltpu.get_barrier_semaphore()
    for m in range(1, X):
        pl.semaphore_signal(barrier, inc=1, device_id=dev(lax.rem(ix + m, X), iy), device_id_type=MESH)
    near = jnp.int32(X - 1)
    for side in (0, 1):
        for dx in (-1, 0, 1):
            there = has_col[side] & row_ok(dx)
            near = near + there.astype(jnp.int32)

            @pl.when(there)
            def _():
                pl.semaphore_signal(
                    barrier, inc=1, device_id=dev(ix + dx, col_partner(side)), device_id_type=MESH
                )

    lane = lanes((LEV, T))
    loads[1].wait()
    for k in range(3):
        for r in range(R):
            parent[k, r] = raw[k, :, r, :]

    a0 = jnp.full((LEV, T), anchor[0], jnp.int32)
    first = (a0 - 1, a0 + (R * X // 2 - 4 - 1))
    in_west = ix <= half + 1
    in_east = ix >= half - 1

    def share_rows(which):
        base = 1 if which else 0

        def one(n, carry):
            t, k = n // 3, lax.rem(n, 3)
            body = jnp.zeros((LEV, T), F32)
            for i in range(R):
                body = jnp.where(first[which] + t == R * ix + i, parent[k, i], body)
            send_w[which, base + n] = body
            return carry

        lax.fori_loop(0, 18, one, 0)

    pl.when(in_west)(lambda: share_rows(WEST))
    pl.when(in_east)(lambda: share_rows(EAST))

    pl.semaphore_wait(barrier, near)

    def pack_copy(side, dx):
        return rcopy(
            edge.at[side], pb.at[1 - dx, 1 - side], pack_ss.at[dx + 1, side], pack_rs.at[1 - dx, 1 - side],
            ix + dx, col_partner(side),
        )

    def ph_copy(down):
        if down:
            return rcopy(parent.at[:, 0], phb.at[1], ph_ss.at[1], ph_rs.at[1], ix - 1, iy)
        return rcopy(parent.at[:, R - 1], phb.at[0], ph_ss.at[0], ph_rs.at[0], ix + 1, iy)

    def halo_copy(down, j):
        if down:
            return rcopy(nest_in.at[:, j], hh.at[:, j], halo_ss.at[1, j], halo_rs.at[1, j], ix - 1, iy)
        i = H - 1 - j
        return rcopy(nest_in.at[:, N - 1 - j], hl.at[:, i], halo_ss.at[0, j], halo_rs.at[0, j], ix + 1, iy)

    def halo_send(down, rows):
        for j in rows:
            halo_copy(down, j).start()

    spans = (((0, 6), (6, 12), (12, 15), (15, 19)), ((13, 19), (7, 13), (4, 7), (0, 4)))

    def window_copy(which, c, x):
        lo, hi = spans[which][c]
        span = pl.ds(lo, hi - lo)
        return rcopy(
            send_w.at[which, span], recv_w.at[which, span], win_ss.at[which, c], win_rs.at[which, c], x, iy
        )

    def window_add(which, c):
        window_copy(which, c, lax.rem(ix + 1, X)).wait_recv()

        def add(n, carry):
            send_w[which, n] = send_w[which, n] + recv_w[which, n]
            return carry

        lax.fori_loop(spans[which][c][0], spans[which][c][1], add, 0)

    @pl.when(ix == half)
    def _():
        for c in range(3):
            window_copy(WEST, c, ix - 1).start()
            if half < X - 1:
                window_copy(EAST, c, ix + 1).start()

    pl.when(ix > 0)(lambda: halo_send(True, (0,)))
    pl.when(ix < X - 1)(lambda: halo_send(False, (0,)))

    loads[0].wait()
    for side in (0, 1):
        packs = jnp.zeros((LEV, T), F32)
        for n in range(3 * N + 3 * R):
            if n < 3 * N:
                v = nest[n // N, n % N, :, C - T : C] if side else nest[n // N, n % N, :, 0:T]
                to = H * n
            else:
                m = n - 3 * N
                v = parent[m // R, m % R]
                to = 64 + H * m
            spot = (lane >= to) & (lane < to + H)
            turn = (to + H * side) % T
            packs = jnp.where(spot, pltpu.roll(v, turn, 1) if turn else v, packs)
        edge[side] = packs

    for dx in (0, -1, 1):
        for side in (0, 1):
            there = has_col[side] & row_ok(dx)
            pl.when(there)(lambda: pack_copy(side, dx).start())
            pl.when(jnp.logical_not(there))(
                lambda: pb.__setitem__((dx + 1, side), jnp.zeros((LEV, T), F32))
            )
    pl.when(ix > 0)(lambda: ph_copy(True).start())
    pl.when(ix < X - 1)(lambda: ph_copy(False).start())
    pl.when(ix > half + 1)(lambda: halo_send(True, (1, 2)))
    pl.when(ix < half - 1)(lambda: halo_send(False, (1, 2)))

    def pack_wait(dx):
        for side in (0, 1):
            pl.when(has_col[side] & row_ok(dx))(
                lambda: arrived(pb.at[dx + 1, side], pack_rs.at[dx + 1, side])
            )

    pack_wait(0)

    rim_spot = (lane < H) | (lane >= T - H)

    def unpack(dx, off):
        left = pltpu.roll(pb[dx + 1, 0], lax.rem(2 * T - H - off, T), 1)
        right = pltpu.roll(pb[dx + 1, 1], lax.rem(T - off, T), 1)
        return jnp.where(rim_spot, jnp.where(lane < T // 2, right, left), 0.0)

    def take_parent(n, carry):
        k, r = n // R, lax.rem(n, R)
        px[k, r + 1, :, 0:T] = parent[k, r]
        px[k, r + 1, :, T : 2 * T] = unpack(0, 64 + H * n)
        return carry

    lax.fori_loop(0, 3 * R, take_parent, 0)

    def share_rims(which):
        acc = jnp.zeros((LEV, T), F32)
        for n in range(18):
            t, k = n // 3, n % 3
            rim = jnp.zeros((LEV, T), F32)
            for i in range(R):
                rim = jnp.where(first[which] + t == R * ix + i, px[k, i + 1, :, T : 2 * T], rim)
            spot = (lane >= 6 * n) & (lane < 6 * n + 6)
            acc = jnp.where(spot, pltpu.roll(rim, (6 * n + H) % T, 1), acc)
        send_w[which, 0 if which else 18] = acc

    pl.when(in_west)(lambda: share_rims(WEST))
    pl.when(in_east)(lambda: share_rims(EAST))

    @pl.when(ix == half + 1)
    def _():
        window_copy(WEST, 3, ix - 1).start()
        halo_send(True, (1, 2))

    @pl.when(ix == half - 1)
    def _():
        window_copy(EAST, 3, ix + 1).start()
        halo_send(False, (1, 2))

    if half > 1:

        @pl.when((ix > 0) & (ix < half))
        def _():
            for c in range(3):
                window_add(WEST, c)
                window_copy(WEST, c, ix - 1).start()

    if half + 1 < X - 1:

        @pl.when((ix > half) & (ix < X - 1))
        def _():
            for c in range(3):
                window_add(EAST, c)
                window_copy(EAST, c, ix + 1).start()

    def take_rows(src, dx, first_row, count, at, only=None):
        def one(n, carry):
            k, r = (n // count, n % count) if only is not None else (n // count, lax.rem(n, count))
            sa[k, at + r, :, 0:C] = src[k, r]
            sa[k, at + r, :, C:W] = unpack(dx, H * (k * N + first_row + r))
            return carry

        if only is None:
            lax.fori_loop(0, 3 * count, one, 0)
        else:
            for k in range(3):
                one(k * count + only, 0)

    take_rows(nest, 0, 0, N, H)

    @pl.when(ix == half)
    def _():
        window_add(WEST, 3)
        window_copy(WEST, 3, ix - 1).start()
        window_add(EAST, 3)
        if half < X - 1:
            window_copy(EAST, 3, ix + 1).start()

    if half > 1:

        @pl.when((ix > 0) & (ix < half))
        def _():
            window_add(WEST, 3)
            window_copy(WEST, 3, ix - 1).start()

    if half + 1 < X - 1:

        @pl.when((ix > half) & (ix < X - 1))
        def _():
            window_add(EAST, 3)
            window_copy(EAST, 3, ix + 1).start()

    pl.when((ix > 0) & (ix <= half))(lambda: halo_send(True, (1, 2)))
    pl.when((ix < X - 1) & (ix >= half))(lambda: halo_send(False, (1, 2)))

    for load in loads[2:5]:
        load.wait()
    diagonal = lanes((LEV, LEV)) == lanes((LEV, LEV), 0)

    def column(ref):
        w = jnp.where(diagonal, jnp.broadcast_to(ref[...], (LEV, LEV)), 0.0)
        return jnp.broadcast_to(0.5 * jnp.sum(w, axis=1, keepdims=True), (LEV, T))

    wind = column(wind_x)
    coef[0] = 0.125 - wind
    coef[1] = 0.125 + wind
    wind = column(wind_y)
    coef[2] = 0.125 - wind
    coef[3] = 0.125 + wind
    mixer[...] = jnp.zeros_like(mixer)
    for i in range(3):
        whole = mix[...]
        top_part = whole.astype(BF16).astype(F32)
        mixer[i, 0:LEV, 0:LEV] = whole - top_part if i == 1 else top_part
    DEEP = mixer.shape[2]
    placed = mixer[0] + pltpu.roll(mixer[1], LEV, 1) + pltpu.roll(mixer[2], 2 * LEV, 1)
    packed[...] = placed.astype(BF16)
    cE, cW, cN, cS = range(4)

    def step(src, r, width):
        wide = width // T

        def cf(i):
            return jnp.concatenate([coef[i]] * wide, axis=1)

        def nb(k):
            x = src[k, r]
            return x, pltpu.roll(x, width - 1, 1), pltpu.roll(x, 1, 1)

        u, un, us = nb(0)
        v, vn, vs = nb(1)
        p, pn, ps = nb(2)

        def adv(k, x, xn, xs):
            return (
                0.5 * x + cf(cE) * src[k, r + 1] + cf(cW) * src[k, r - 1] + cf(cN) * xn + cf(cS) * xs
            )

        fu = adv(0, u, un, us) - 0.3 * (src[2, r + 1] - src[2, r - 1])
        fv = adv(1, v, vn, vs) - 0.3 * (pn - ps)
        fp = adv(2, p, pn, ps) - 0.3 * (src[0, r + 1] - src[0, r - 1] + (vn - vs))
        outs = []
        for f in (fu, fv, fp):
            hi = f.astype(BF16).astype(F32)
            stacked = jnp.concatenate([hi, hi, f - hi], axis=0)
            if DEEP > 3 * LEV:
                stacked = jnp.concatenate([stacked, jnp.zeros((DEEP - 3 * LEV, width), F32)], axis=0)
            mixed = jnp.dot(packed[...], stacked.astype(BF16), preferred_element_type=F32)
            outs.append(f + mixed[:LEV])
        return outs

    @pl.when(ix > 0)
    def _():
        arrived(phb.at[0], ph_rs.at[0])

    @pl.when(ix < X - 1)
    def _():
        arrived(phb.at[1], ph_rs.at[1])

    pl.when(ix == 0)(lambda: phb.__setitem__(0, jnp.zeros((3, LEV, T), F32)))
    pl.when(ix == X - 1)(lambda: phb.__setitem__(1, jnp.zeros((3, LEV, T), F32)))
    for k in range(3):
        px[k, 0, :, 0:T] = phb[0, k]
        px[k, R + 1, :, 0:T] = phb[1, k]
        px[k, 0, :, T : 2 * T] = jnp.zeros((LEV, T), F32)
        px[k, R + 1, :, T : 2 * T] = jnp.zeros((LEV, T), F32)

    def parent_row(r, carry):
        for k, f in enumerate(step(px, r + 1, 2 * T)):
            parent_out[k, r] = f[:, 0:T]
        return carry

    lax.fori_loop(0, R, parent_row, 0)

    def masked(f, width):
        at = lanes((1, T))
        off_left = ((at >= T // 2) & (iy == 0)) | ((at < T // 2) & (iy == Y - 1))
        tail = jnp.where(off_left, 0.0, f[:, width - T : width])
        return jnp.concatenate([f[:, 0 : width - T], tail], axis=1)

    def run(src, dst, lo, hi):
        def one(r, carry):
            for k, f in enumerate(step(src, r, W)):
                dst[k, r] = masked(f, W)
            return carry

        lax.fori_loop(lo, hi, one, 0)

    def run_out(r):
        for k, f in enumerate(step(sa, r, W)):
            nest_out[k, r - H] = f[:, 0:C]

    top = N + 2 * H
    at_w, at_e = H + 3, H + N - 4
    outer = is_west | is_east
    inner = jnp.logical_not(outer)
    run(sa, sb, jnp.where(is_west, at_w + 1, H + 1), jnp.where(is_east, at_e, H + N - 1))

    @pl.when(inner)
    def _():
        run(sb, sa, H + 2, H + N - 2)

    e = jnp.where(is_west, 0, 1)
    b_adj = jnp.where(is_west, 3, 0)

    def wt_copy(side):
        src = wx.at[:, :, C - T : C] if side else wx.at[:, :, 0:T]
        return rcopy(src, wrb.at[1 - side], wt_ss.at[side], wt_rs.at[1 - side], ix, col_partner(side))

    for load in loads[5:]:
        load.wait()

    @pl.when(outer)
    def _():
        for row in range(4):
            for dc in range(3):
                acc = jnp.zeros((4, C), F32)
                for n in range(4):
                    hit = (d_rows[n, e] == row) & (d_cols[n, e] == dc - 1)
                    acc = acc + jnp.where(hit, d_wts[n, e], 0.0)
                wx[row * 3 + dc] = acc
        for side in (0, 1):
            pl.when(has_col[side])(lambda: wt_copy(side).start())
            pl.when(jnp.logical_not(has_col[side]))(
                lambda: wrb.__setitem__(side, jnp.zeros((12, 4, T), F32))
            )

    def take(j, low):
        if low:
            arrived(hl.at[:, H - 1 - j], halo_rs.at[0, j])
            take_rows(hl, -1, N - H, H, 0, H - 1 - j)
        else:
            arrived(hh.at[:, j], halo_rs.at[1, j])
            take_rows(hh, 1, 0, H, H + N, j)

    def at(j, s, low):
        return H - j + s - 1 if low else H + N - 1 + j - s + 1

    def one_row(src, dst, r):
        run(src, dst, r, r + 1)

    def grow(j, low):
        one_row(sa, sb, at(j, 1, low))
        one_row(sb, sa, at(j, 2, low))
        run_out(at(j, 3, low))

    @pl.when(ix > 0)
    def _():
        pack_wait(-1)
        take(0, True)
        one_row(sa, sb, at(0, 1, True))

    @pl.when(ix < X - 1)
    def _():
        pack_wait(1)
        take(0, False)
        one_row(sa, sb, at(0, 1, False))

    @pl.when(outer)
    def _():
        for side in (0, 1):
            pl.when(has_col[side])(lambda: arrived(wrb.at[side], wt_rs.at[side]))
        at8 = lanes((8, T))
        for b in range(4):
            for i in range(12):
                left = jnp.broadcast_to(wrb[0, i, b : b + 1, :], (8, T))
                right = jnp.broadcast_to(wrb[1, i, b : b + 1, :], (8, T))
                wxb[i, b, :, 0:C] = jnp.broadcast_to(wx[i, b : b + 1, :], (8, C))
                wxb[i, b, :, C:W] = jnp.where(at8 < T // 2, right, left)

        y = lanes((2 * T, W))
        c = lanes((2 * T, W), 0)
        y = jnp.where(y < C + T // 2, y, y - W)
        c = jnp.where(c < T + T // 2, c, c - 2 * T)
        for dc in range(3):
            gap = y - 3 * (c - (dc - 1))
            hot[dc] = jnp.where((gap >= 0) & (gap <= 2), 1.0, 0.0).astype(BF16)

    def edge_work(which):
        base = 1 if which else 0
        rims = 0 if which else 18
        for c in range(4):
            window_add(which, c)

        def lay(n, carry):
            t, k = n // 3, lax.rem(n, 3)
            zb[k, t, :, 0:T] = send_w[which, base + n]
            tail = pltpu.roll(send_w[which, rims], lax.rem(2 * T - 6 * n - H, T), 1)
            zb[k, t, :, T : 2 * T] = jnp.where(rim_spot, tail, 0.0)
            return carry

        lax.fori_loop(0, 18, lay, 0)

    pl.when(is_west)(lambda: edge_work(WEST))
    pl.when(is_east)(lambda: edge_work(EAST))

    @pl.when(outer)
    def _():
        def zone_row(r, carry):
            for k, f in enumerate(step(zb, r + 1, 2 * T)):
                zn[k, r] = masked(f, 2 * T)
            return carry

        lax.fori_loop(0, 4, zone_row, 0)
        for dc in range(3):

            def spread(k, carry):
                for time in range(2):
                    rows = zn[k] if time else zb[k, 1:5]
                    hi, lo = split(rows.reshape(4 * LEV, 2 * T))
                    got = jnp.dot(hi, hot[dc], preferred_element_type=F32) + jnp.dot(
                        lo, hot[dc], preferred_element_type=F32
                    )
                    grid[time, k, dc] = got.reshape(4, LEV, W)
                return carry

            lax.fori_loop(0, 3, spread, 0)

        def bound(time, k, b):
            acc = jnp.zeros((LEV, W), F32)
            for row in range(4):
                for dc in range(3):
                    w = jnp.concatenate([wxb[row * 3 + dc, b]] * (LEV // 8), axis=0)
                    acc = acc + w * grid[time, k, dc, row]
            return acc

        def each(n, carry):
            k, b = n // 4, lax.rem(n, 4)
            got = bound(1, k, b)
            b1[b, k] = got
            nest_out[k, jnp.where(is_west, 0, N - 4) + b] = got[:, 0:C]
            return carry

        lax.fori_loop(0, 12, each, 0)

        def each0(k, carry):
            b0[k] = bound(0, k, b_adj)
            return carry

        lax.fori_loop(0, 3, each0, 0)

        ra = jnp.where(is_west, at_w, at_e)
        for k in range(3):
            sb[k, ra] = (1.0 - 1.0 / 3.0) * b0[k] + (1.0 / 3.0) * b1[b_adj, k]
            sa[k, ra] = (1.0 - 2.0 / 3.0) * b0[k] + (2.0 / 3.0) * b1[b_adj, k]

    @pl.when(ix > 0)
    def _():
        one_row(sb, sa, at(0, 2, True))
        pl.when(inner)(lambda: run_out(at(0, 3, True)))

    @pl.when(ix < X - 1)
    def _():
        one_row(sb, sa, at(0, 2, False))
        pl.when(inner)(lambda: run_out(at(0, 3, False)))

    for low in (True, False):

        @pl.when(ix > 0 if low else ix < X - 1)
        def _():
            for j in (1, 2):
                take(j, low)
                grow(j, low)

    per = N // 3
    sums = []
    for g in range(per):
        for k in range(3):
            sums.append(nest_out[k, 3 * g] + nest_out[k, 3 * g + 1] + nest_out[k, 3 * g + 2])
    hi, lo = split(jnp.concatenate(sums, axis=0))
    gap = lanes((C, T), 0) - 3 * lanes((C, T))
    pool = jnp.where((gap >= 0) & (gap <= 2), 1.0, 0.0).astype(BF16)
    mean = jnp.dot(hi, pool, preferred_element_type=F32) + jnp.dot(lo, pool, preferred_element_type=F32)
    co[...] = (mean * (1.0 / 9.0)).reshape(per, 3, LEV, T)

    def co_copy(g, m):
        return rcopy(co.at[g], cb.at[per * ix + g], co_ss.at[m, g], co_rs.at[per * ix + g], 1 + ix // 2 + m, iy)

    def co_each(action):
        for m in range(half):
            for g in range(per):
                inner = jnp.logical_not(is_west) if g == 0 else jnp.logical_not(is_east)
                pl.when(inner & (1 + ix // 2 + m != ix))(lambda: action(co_copy(g, m)))

    co_each(lambda copy: copy.start())

    def put(src, g):
        for i in range(R):
            hit = a0 + g == R * ix + i
            for k in range(3):
                parent_out[k, i] = jnp.where(hit, src[k], parent_out[k, i])

    def feed(g, carry):
        j = g // per
        reach = (1 + j // 2 <= ix) & (ix <= half + j // 2)

        @pl.when(reach & (j != ix))
        def _():
            arrived(cb.at[g], co_rs.at[g])
            put(cb.at[g], g)

        @pl.when(reach & (j == ix))
        def _():
            put(co.at[lax.rem(g, per)], g)

        return carry

    lax.fori_loop(1, per * X - 1, feed, 0)

    for dx in (0, -1, 1):
        for side in (0, 1):
            pl.when(has_col[side] & row_ok(dx))(lambda: pack_copy(side, dx).wait_send())
    pl.when(ix > 0)(lambda: ph_copy(True).wait_send())
    pl.when(ix < X - 1)(lambda: ph_copy(False).wait_send())
    for j in range(H):
        pl.when(ix > 0)(lambda: halo_copy(True, j).wait_send())
        pl.when(ix < X - 1)(lambda: halo_copy(False, j).wait_send())
    pl.when(ix == half + 1)(lambda: window_copy(WEST, 3, ix - 1).wait_send())
    pl.when(ix == half - 1)(lambda: window_copy(EAST, 3, ix + 1).wait_send())
    for c in range(4):
        pl.when((ix > 0) & (ix <= half))(lambda: window_copy(WEST, c, ix - 1).wait_send())
        pl.when((ix >= half) & (ix < X - 1))(lambda: window_copy(EAST, c, ix + 1).wait_send())
    for side in (0, 1):
        pl.when(outer & has_col[side])(lambda: wt_copy(side).wait_send())
    co_each(lambda copy: copy.wait_send())


def shards(parent, nest, nest_anchor, donor_rows, donor_cols, donor_weights, wind_x, wind_y, column_mix):
    X = lax.axis_size("gx")
    CY = lax.axis_size("gz")
    Y = lax.axis_size("gy") * CY
    LEV, R = parent.shape[1], parent.shape[2]
    N, C = nest.shape[2], nest.shape[3]
    W = C + T
    top = N + 2 * H
    per = N // 3
    deep = -(-3 * LEV // T) * T
    LEVP = -(-LEV // 16) * 16
    vmem = pl.BlockSpec(memory_space=pltpu.VMEM)
    hbm = pl.BlockSpec(memory_space=pltpu.HBM)
    smem = pl.BlockSpec(memory_space=pltpu.SMEM)
    V = lambda *s: pltpu.VMEM(s, F32)
    I = lambda *s: pltpu.VMEM(s, jnp.int32)
    D = lambda *s: pltpu.SemaphoreType.DMA(s)
    outs = pl.pallas_call(
        functools.partial(kernel, X, Y, CY),
        out_shape=(
            jax.ShapeDtypeStruct((3, R, LEV, T), F32),
            jax.ShapeDtypeStruct((3, N, LEV, C), F32),
        ),
        in_specs=[hbm, hbm, smem, hbm, hbm, hbm, hbm, hbm, hbm],
        out_specs=(vmem, vmem),
        scratch_shapes=[
            V(3, LEV, R, T),
            V(3, N, LEV, C),
            I(4, 2, 4, C),
            I(4, 2, 4, C),
            V(4, 2, 4, C),
            V(1, LEV),
            V(1, LEV),
            V(LEV, LEV),
            V(3, R, LEV, T),
            V(4, LEV, T),
            V(3, LEVP, deep),
            pltpu.VMEM((LEVP, deep), BF16),
            pltpu.VMEM((3, 2 * T, W), BF16),
            V(2, LEV, T),
            V(3, 2, LEV, T),
            V(2, 3, LEV, T),
            V(3, H, LEV, C),
            V(3, H, LEV, C),
            V(3, R + 2, LEV, 2 * T),
            V(3, top, LEV, W),
            V(3, top, LEV, W),
            V(2, 19, LEV, T),
            V(2, 19, LEV, T),
            V(3, 6, LEV, 2 * T),
            V(3, 4, LEV, 2 * T),
            V(2, 3, 3, 4, LEV, W),
            V(12, 4, C),
            V(2, 12, 4, T),
            V(12, 4, 8, W),
            V(3, LEV, W),
            V(4, 3, LEV, W),
            V(per, 3, LEV, T),
            V(per * X, 3, LEV, T),
            D(8),
            D(3, 2), D(3, 2), D(2), D(2), D(2, H), D(2, H), D(2, 4), D(2, 4), D(2), D(2), D(X // 2, per), D(per * X),
        ],
        compiler_params=pltpu.CompilerParams(
            collective_id=0, has_side_effects=True, vmem_limit_bytes=62 * 1024 * 1024
        ),
        cost_estimate=pl.CostEstimate(flops=200_000_000, bytes_accessed=6_000_000, transcendentals=0),
    )(
        parent,
        nest.transpose(0, 2, 1, 3),
        nest_anchor,
        donor_rows,
        donor_cols,
        donor_weights,
        wind_x.reshape(1, LEV),
        wind_y.reshape(1, LEV),
        column_mix,
    )
    return tuple(x.transpose(0, 2, 1, 3) for x in outs)


def solution(mesh):
    grids = P("member", None, "gx", ("gy", "gz"))
    donors = P("member", None, None, ("gy", "gz"))
    return jax.shard_map(
        shards,
        mesh=mesh,
        in_specs=(grids, grids, P("member"), donors, donors, donors, P(), P(), P()),
        out_specs=(grids, grids),
        check_vma=False,
    )
```

```python
import functools

import jax
import jax.numpy as jnp
from jax import lax
from jax.experimental import pallas as pl
from jax.experimental.pallas import tpu as pltpu
from jax.sharding import PartitionSpec as P

MESH = pl.DeviceIdType.MESH
F32 = jnp.float32
BF16 = jnp.bfloat16
T = 128
H = 3
WEST, EAST = 0, 1


def lanes(shape, dim=1):
    return lax.broadcasted_iota(jnp.int32, shape, dim)


def split(x):
    hi = x.astype(BF16)
    lo = (x - hi.astype(F32)).astype(BF16)
    return hi, lo


def kernel(
    X, Y, CY,
    parent_in, nest_in, anchor, rows_in, cols_in, wts_in, wind_x_in, wind_y_in, mix_in,
    parent_out, nest_out,
    raw, nest, d_rows, d_cols, d_wts, wind_x, wind_y, mix, parent, coef, mixer, packed, hot,
    edge, pb, phb, hl, hh, px, sa, sb, send_w, recv_w, zb, zn, grid, wx, wrb, wxb, b0, b1, co, cb, load_s,
    pack_ss, pack_rs, ph_ss, ph_rs, halo_ss, halo_rs, win_ss, win_rs, wt_ss, wt_rs, co_ss, co_rs,
):
    pairs = (
        (nest_in, nest), (parent_in, raw), (wind_x_in, wind_x), (wind_y_in, wind_y), (mix_in, mix),
        (rows_in, d_rows), (cols_in, d_cols), (wts_in, d_wts),
    )
    loads = [pltpu.make_async_copy(a, b, load_s.at[i]) for i, (a, b) in enumerate(pairs)]
    for load in loads:
        load.start()
    R = parent.shape[1]
    N = nest.shape[1]
    LEV = nest.shape[2]
    C = nest.shape[3]
    W = C + T
    me = lax.axis_index("member")
    ix = lax.axis_index("gx")
    iy = lax.axis_index("gy") * CY + lax.axis_index("gz")
    half = X // 2
    is_west = ix == 0
    is_east = ix == X - 1
    has_col = (iy > 0, iy < Y - 1)

    def dev(x, y):
        return (me, x, y // CY, lax.rem(y, CY))

    def rcopy(src, dst, ss, rs, x, y):
        return pltpu.make_async_remote_copy(
            src_ref=src, dst_ref=dst, send_sem=ss, recv_sem=rs, device_id=dev(x, y), device_id_type=MESH
        )

    def arrived(ref, rs):
        rcopy(ref, ref, halo_ss.at[0, 0], rs, lax.rem(ix + 1, X), iy).wait_recv()

    def col_partner(side):
        return iy + (1 if side else -1)

    def row_ok(dx):
        return (ix + dx >= 0) & (ix + dx < X)

    barrier = pltpu.get_barrier_semaphore()
    for m in range(1, X):
        pl.semaphore_signal(barrier, inc=1, device_id=dev(lax.rem(ix + m, X), iy), device_id_type=MESH)
    near = jnp.int32(X - 1)
    for side in (0, 1):
        for dx in (-1, 0, 1):
            there = has_col[side] & row_ok(dx)
            near = near + there.astype(jnp.int32)

            @pl.when(there)
            def _():
                pl.semaphore_signal(
                    barrier, inc=1, device_id=dev(ix + dx, col_partner(side)), device_id_type=MESH
                )

    lane = lanes((LEV, T))
    loads[1].wait()
    for k in range(3):
        for r in range(R):
            parent[k, r] = raw[k, :, r, :]

    a0 = jnp.full((LEV, T), anchor[0], jnp.int32)
    first = (a0 - 1, a0 + (R * X // 2 - 4 - 1))
    in_west = ix <= half + 1
    in_east = ix >= half - 1

    def share_rows(which):
        base = 1 if which else 0

        def one(n, carry):
            t, k = n // 3, lax.rem(n, 3)
            body = jnp.zeros((LEV, T), F32)
            for i in range(R):
                body = jnp.where(first[which] + t == R * ix + i, parent[k, i], body)
            send_w[which, base + n] = body
            return carry

        lax.fori_loop(0, 18, one, 0)

    pl.when(in_west)(lambda: share_rows(WEST))
    pl.when(in_east)(lambda: share_rows(EAST))

    loads[0].wait()
    for side in (0, 1):
        packs = jnp.zeros((LEV, T), F32)
        for n in range(3 * N + 3 * R):
            if n < 3 * N:
                v = nest[n // N, n % N, :, C - T : C] if side else nest[n // N, n % N, :, 0:T]
                to = H * n
            else:
                m = n - 3 * N
                v = parent[m // R, m % R]
                to = 64 + H * m
            spot = (lane >= to) & (lane < to + H)
            turn = (to + H * side) % T
            packs = jnp.where(spot, pltpu.roll(v, turn, 1) if turn else v, packs)
        edge[side] = packs

    pl.semaphore_wait(barrier, near)

    def pack_copy(side, dx):
        return rcopy(
            edge.at[side], pb.at[1 - dx, 1 - side], pack_ss.at[dx + 1, side], pack_rs.at[1 - dx, 1 - side],
            ix + dx, col_partner(side),
        )

    def ph_copy(down):
        if down:
            return rcopy(parent.at[:, 0], phb.at[1], ph_ss.at[1], ph_rs.at[1], ix - 1, iy)
        return rcopy(parent.at[:, R - 1], phb.at[0], ph_ss.at[0], ph_rs.at[0], ix + 1, iy)

    def halo_copy(down, j):
        if down:
            return rcopy(nest_in.at[:, j], hh.at[:, j], halo_ss.at[1, j], halo_rs.at[1, j], ix - 1, iy)
        i = H - 1 - j
        return rcopy(nest_in.at[:, N - 1 - j], hl.at[:, i], halo_ss.at[0, j], halo_rs.at[0, j], ix + 1, iy)

    def halo_send(down, rows):
        for j in rows:
            halo_copy(down, j).start()

    spans = (((0, 6), (6, 12), (12, 15), (15, 19)), ((13, 19), (7, 13), (4, 7), (0, 4)))

    def window_copy(which, c, x):
        lo, hi = spans[which][c]
        span = pl.ds(lo, hi - lo)
        return rcopy(
            send_w.at[which, span], recv_w.at[which, span], win_ss.at[which, c], win_rs.at[which, c], x, iy
        )

    def window_add(which, c):
        window_copy(which, c, lax.rem(ix + 1, X)).wait_recv()

        def add(n, carry):
            send_w[which, n] = send_w[which, n] + recv_w[which, n]
            return carry

        lax.fori_loop(spans[which][c][0], spans[which][c][1], add, 0)

    for dx in (0, -1, 1):
        for side in (0, 1):
            there = has_col[side] & row_ok(dx)
            pl.when(there)(lambda: pack_copy(side, dx).start())
            pl.when(jnp.logical_not(there))(
                lambda: pb.__setitem__((dx + 1, side), jnp.zeros((LEV, T), F32))
            )
    pl.when(ix > 0)(lambda: ph_copy(True).start())
    pl.when(ix < X - 1)(lambda: ph_copy(False).start())
    @pl.when(ix == half)
    def _():
        for c in range(3):
            window_copy(WEST, c, ix - 1).start()
            if half < X - 1:
                window_copy(EAST, c, ix + 1).start()

    starter = (ix == half + 1) | (ix == half - 1)
    pl.when((ix > 0) & jnp.logical_not(starter))(lambda: halo_send(True, (0,)))
    pl.when((ix < X - 1) & jnp.logical_not(starter))(lambda: halo_send(False, (0,)))
    pl.when(ix > half + 1)(lambda: halo_send(True, (1, 2)))
    pl.when(ix < half - 1)(lambda: halo_send(False, (1, 2)))

    def pack_wait(dx):
        for side in (0, 1):
            pl.when(has_col[side] & row_ok(dx))(
                lambda: arrived(pb.at[dx + 1, side], pack_rs.at[dx + 1, side])
            )

    pack_wait(0)

    rim_spot = (lane < H) | (lane >= T - H)

    def unpack(dx, off):
        left = pltpu.roll(pb[dx + 1, 0], lax.rem(2 * T - H - off, T), 1)
        right = pltpu.roll(pb[dx + 1, 1], lax.rem(T - off, T), 1)
        return jnp.where(rim_spot, jnp.where(lane < T // 2, right, left), 0.0)

    def take_parent(n, carry):
        k, r = n // R, lax.rem(n, R)
        px[k, r + 1, :, 0:T] = parent[k, r]
        px[k, r + 1, :, T : 2 * T] = unpack(0, 64 + H * n)
        return carry

    lax.fori_loop(0, 3 * R, take_parent, 0)

    def share_rims(which):
        acc = jnp.zeros((LEV, T), F32)
        for n in range(18):
            t, k = n // 3, n % 3
            rim = jnp.zeros((LEV, T), F32)
            for i in range(R):
                rim = jnp.where(first[which] + t == R * ix + i, px[k, i + 1, :, T : 2 * T], rim)
            spot = (lane >= 6 * n) & (lane < 6 * n + 6)
            acc = jnp.where(spot, pltpu.roll(rim, (6 * n + H) % T, 1), acc)
        send_w[which, 0 if which else 18] = acc

    pl.when(in_west)(lambda: share_rims(WEST))
    pl.when(in_east)(lambda: share_rims(EAST))

    @pl.when(ix == half + 1)
    def _():
        window_copy(WEST, 3, ix - 1).start()
        halo_send(True, (0, 1, 2))
        pl.when(ix < X - 1)(lambda: halo_send(False, (0,)))

    @pl.when(ix == half - 1)
    def _():
        window_copy(EAST, 3, ix + 1).start()
        pl.when(ix > 0)(lambda: halo_send(True, (0,)))
        halo_send(False, (0, 1, 2))

    if half > 1:

        @pl.when((ix > 0) & (ix < half))
        def _():
            for c in range(3):
                window_add(WEST, c)
                window_copy(WEST, c, ix - 1).start()

    if half + 1 < X - 1:

        @pl.when((ix > half) & (ix < X - 1))
        def _():
            for c in range(3):
                window_add(EAST, c)
                window_copy(EAST, c, ix + 1).start()

    def take_rows(src, dx, first_row, count, at, only=None):
        def one(n, carry):
            k, r = (n // count, n % count) if only is not None else (n // count, lax.rem(n, count))
            sa[k, at + r, :, 0:C] = src[k, r]
            sa[k, at + r, :, C:W] = unpack(dx, H * (k * N + first_row + r))
            return carry

        if only is None:
            lax.fori_loop(0, 3 * count, one, 0)
        else:
            for k in range(3):
                one(k * count + only, 0)

    take_rows(nest, 0, 0, N, H)

    @pl.when(ix == half)
    def _():
        window_add(WEST, 3)
        window_copy(WEST, 3, ix - 1).start()
        window_add(EAST, 3)
        if half < X - 1:
            window_copy(EAST, 3, ix + 1).start()

    if half > 1:

        @pl.when((ix > 0) & (ix < half))
        def _():
            window_add(WEST, 3)
            window_copy(WEST, 3, ix - 1).start()

    if half + 1 < X - 1:

        @pl.when((ix > half) & (ix < X - 1))
        def _():
            window_add(EAST, 3)
            window_copy(EAST, 3, ix + 1).start()

    pl.when((ix > 0) & (ix <= half))(lambda: halo_send(True, (1, 2)))
    pl.when((ix < X - 1) & (ix >= half))(lambda: halo_send(False, (1, 2)))

    for load in loads[2:5]:
        load.wait()
    diagonal = lanes((LEV, LEV)) == lanes((LEV, LEV), 0)

    def column(ref):
        w = jnp.where(diagonal, jnp.broadcast_to(ref[...], (LEV, LEV)), 0.0)
        return jnp.broadcast_to(0.5 * jnp.sum(w, axis=1, keepdims=True), (LEV, T))

    wind = column(wind_x)
    coef[0] = 0.125 - wind
    coef[1] = 0.125 + wind
    wind = column(wind_y)
    coef[2] = 0.125 - wind
    coef[3] = 0.125 + wind
    mixer[...] = jnp.zeros_like(mixer)
    for i in range(3):
        whole = mix[...]
        top_part = whole.astype(BF16).astype(F32)
        mixer[i, 0:LEV, 0:LEV] = whole - top_part if i == 1 else top_part
    DEEP = mixer.shape[2]
    placed = mixer[0] + pltpu.roll(mixer[1], LEV, 1) + pltpu.roll(mixer[2], 2 * LEV, 1)
    packed[...] = placed.astype(BF16)
    cE, cW, cN, cS = range(4)

    def step(src, r, width):
        wide = width // T

        def cf(i):
            return jnp.concatenate([coef[i]] * wide, axis=1)

        def nb(k):
            x = src[k, r]
            return x, pltpu.roll(x, width - 1, 1), pltpu.roll(x, 1, 1)

        u, un, us = nb(0)
        v, vn, vs = nb(1)
        p, pn, ps = nb(2)

        def adv(k, x, xn, xs):
            return (
                0.5 * x + cf(cE) * src[k, r + 1] + cf(cW) * src[k, r - 1] + cf(cN) * xn + cf(cS) * xs
            )

        fu = adv(0, u, un, us) - 0.3 * (src[2, r + 1] - src[2, r - 1])
        fv = adv(1, v, vn, vs) - 0.3 * (pn - ps)
        fp = adv(2, p, pn, ps) - 0.3 * (src[0, r + 1] - src[0, r - 1] + (vn - vs))
        outs = []
        for f in (fu, fv, fp):
            hi = f.astype(BF16).astype(F32)
            stacked = jnp.concatenate([hi, hi, f - hi], axis=0)
            if DEEP > 3 * LEV:
                stacked = jnp.concatenate([stacked, jnp.zeros((DEEP - 3 * LEV, width), F32)], axis=0)
            mixed = jnp.dot(packed[...], stacked.astype(BF16), preferred_element_type=F32)
            outs.append(f + mixed[:LEV])
        return outs

    @pl.when(ix > 0)
    def _():
        arrived(phb.at[0], ph_rs.at[0])

    @pl.when(ix < X - 1)
    def _():
        arrived(phb.at[1], ph_rs.at[1])

    pl.when(ix == 0)(lambda: phb.__setitem__(0, jnp.zeros((3, LEV, T), F32)))
    pl.when(ix == X - 1)(lambda: phb.__setitem__(1, jnp.zeros((3, LEV, T), F32)))
    for k in range(3):
        px[k, 0, :, 0:T] = phb[0, k]
        px[k, R + 1, :, 0:T] = phb[1, k]
        px[k, 0, :, T : 2 * T] = jnp.zeros((LEV, T), F32)
        px[k, R + 1, :, T : 2 * T] = jnp.zeros((LEV, T), F32)

    def parent_row(r, carry):
        for k, f in enumerate(step(px, r + 1, 2 * T)):
            parent_out[k, r] = f[:, 0:T]
        return carry

    lax.fori_loop(0, R, parent_row, 0)

    def masked(f, width):
        at = lanes((1, T))
        off_left = ((at >= T // 2) & (iy == 0)) | ((at < T // 2) & (iy == Y - 1))
        tail = jnp.where(off_left, 0.0, f[:, width - T : width])
        return jnp.concatenate([f[:, 0 : width - T], tail], axis=1)

    def run(src, dst, lo, hi):
        def one(r, carry):
            for k, f in enumerate(step(src, r, W)):
                dst[k, r] = masked(f, W)
            return carry

        lax.fori_loop(lo, hi, one, 0)

    def run_out(r):
        for k, f in enumerate(step(sa, r, W)):
            nest_out[k, r - H] = f[:, 0:C]

    top = N + 2 * H
    at_w, at_e = H + 3, H + N - 4
    outer = is_west | is_east
    inner = jnp.logical_not(outer)
    run(sa, sb, jnp.where(is_west, at_w + 1, H + 1), jnp.where(is_east, at_e, H + N - 1))

    @pl.when(inner)
    def _():
        run(sb, sa, H + 2, H + N - 2)

    e = jnp.where(is_west, 0, 1)
    b_adj = jnp.where(is_west, 3, 0)

    def wt_copy(side):
        src = wx.at[:, :, C - T : C] if side else wx.at[:, :, 0:T]
        return rcopy(src, wrb.at[1 - side], wt_ss.at[side], wt_rs.at[1 - side], ix, col_partner(side))

    for load in loads[5:]:
        load.wait()

    @pl.when(outer)
    def _():
        for row in range(4):
            for dc in range(3):
                acc = jnp.zeros((4, C), F32)
                for n in range(4):
                    hit = (d_rows[n, e] == row) & (d_cols[n, e] == dc - 1)
                    acc = acc + jnp.where(hit, d_wts[n, e], 0.0)
                wx[row * 3 + dc] = acc
        for side in (0, 1):
            pl.when(has_col[side])(lambda: wt_copy(side).start())
            pl.when(jnp.logical_not(has_col[side]))(
                lambda: wrb.__setitem__(side, jnp.zeros((12, 4, T), F32))
            )

    def take(j, low):
        if low:
            arrived(hl.at[:, H - 1 - j], halo_rs.at[0, j])
            take_rows(hl, -1, N - H, H, 0, H - 1 - j)
        else:
            arrived(hh.at[:, j], halo_rs.at[1, j])
            take_rows(hh, 1, 0, H, H + N, j)

    def at(j, s, low):
        return H - j + s - 1 if low else H + N - 1 + j - s + 1

    def one_row(src, dst, r):
        run(src, dst, r, r + 1)

    def grow(j, low):
        one_row(sa, sb, at(j, 1, low))
        one_row(sb, sa, at(j, 2, low))
        run_out(at(j, 3, low))

    @pl.when(ix > 0)
    def _():
        pack_wait(-1)
        take(0, True)
        one_row(sa, sb, at(0, 1, True))

    @pl.when(ix < X - 1)
    def _():
        pack_wait(1)
        take(0, False)
        one_row(sa, sb, at(0, 1, False))

    @pl.when(outer)
    def _():
        for side in (0, 1):
            pl.when(has_col[side])(lambda: arrived(wrb.at[side], wt_rs.at[side]))
        at8 = lanes((8, T))
        for b in range(4):
            for i in range(12):
                left = jnp.broadcast_to(wrb[0, i, b : b + 1, :], (8, T))
                right = jnp.broadcast_to(wrb[1, i, b : b + 1, :], (8, T))
                wxb[i, b, :, 0:C] = jnp.broadcast_to(wx[i, b : b + 1, :], (8, C))
                wxb[i, b, :, C:W] = jnp.where(at8 < T // 2, right, left)

        y = lanes((2 * T, W))
        c = lanes((2 * T, W), 0)
        y = jnp.where(y < C + T // 2, y, y - W)
        c = jnp.where(c < T + T // 2, c, c - 2 * T)
        for dc in range(3):
            gap = y - 3 * (c - (dc - 1))
            hot[dc] = jnp.where((gap >= 0) & (gap <= 2), 1.0, 0.0).astype(BF16)

    def edge_work(which):
        base = 1 if which else 0
        rims = 0 if which else 18
        for c in range(4):
            window_add(which, c)

        def lay(n, carry):
            t, k = n // 3, lax.rem(n, 3)
            zb[k, t, :, 0:T] = send_w[which, base + n]
            tail = pltpu.roll(send_w[which, rims], lax.rem(2 * T - 6 * n - H, T), 1)
            zb[k, t, :, T : 2 * T] = jnp.where(rim_spot, tail, 0.0)
            return carry

        lax.fori_loop(0, 18, lay, 0)

    pl.when(is_west)(lambda: edge_work(WEST))
    pl.when(is_east)(lambda: edge_work(EAST))

    @pl.when(outer)
    def _():
        def zone_row(r, carry):
            for k, f in enumerate(step(zb, r + 1, 2 * T)):
                zn[k, r] = masked(f, 2 * T)
            return carry

        lax.fori_loop(0, 4, zone_row, 0)
        for dc in range(3):

            def spread(k, carry):
                for time in range(2):
                    rows = zn[k] if time else zb[k, 1:5]
                    hi, lo = split(rows.reshape(4 * LEV, 2 * T))
                    got = jnp.dot(hi, hot[dc], preferred_element_type=F32) + jnp.dot(
                        lo, hot[dc], preferred_element_type=F32
                    )
                    grid[time, k, dc] = got.reshape(4, LEV, W)
                return carry

            lax.fori_loop(0, 3, spread, 0)

        def bound(time, k, b):
            acc = jnp.zeros((LEV, W), F32)
            for row in range(4):
                for dc in range(3):
                    w = jnp.concatenate([wxb[row * 3 + dc, b]] * (LEV // 8), axis=0)
                    acc = acc + w * grid[time, k, dc, row]
            return acc

        def each(n, carry):
            k, b = n // 4, lax.rem(n, 4)
            got = bound(1, k, b)
            b1[b, k] = got
            nest_out[k, jnp.where(is_west, 0, N - 4) + b] = got[:, 0:C]
            return carry

        lax.fori_loop(0, 12, each, 0)

        def each0(k, carry):
            b0[k] = bound(0, k, b_adj)
            return carry

        lax.fori_loop(0, 3, each0, 0)

        ra = jnp.where(is_west, at_w, at_e)
        for k in range(3):
            sb[k, ra] = (1.0 - 1.0 / 3.0) * b0[k] + (1.0 / 3.0) * b1[b_adj, k]
            sa[k, ra] = (1.0 - 2.0 / 3.0) * b0[k] + (2.0 / 3.0) * b1[b_adj, k]

    @pl.when(ix > 0)
    def _():
        one_row(sb, sa, at(0, 2, True))
        pl.when(inner)(lambda: run_out(at(0, 3, True)))

    @pl.when(ix < X - 1)
    def _():
        one_row(sb, sa, at(0, 2, False))
        pl.when(inner)(lambda: run_out(at(0, 3, False)))

    for low in (True, False):

        @pl.when(ix > 0 if low else ix < X - 1)
        def _():
            for j in (1, 2):
                take(j, low)
                grow(j, low)

    per = N // 3
    sums = []
    for g in range(per):
        for k in range(3):
            sums.append(nest_out[k, 3 * g] + nest_out[k, 3 * g + 1] + nest_out[k, 3 * g + 2])
    hi, lo = split(jnp.concatenate(sums, axis=0))
    gap = lanes((C, T), 0) - 3 * lanes((C, T))
    pool = jnp.where((gap >= 0) & (gap <= 2), 1.0, 0.0).astype(BF16)
    mean = jnp.dot(hi, pool, preferred_element_type=F32) + jnp.dot(lo, pool, preferred_element_type=F32)
    co[...] = (mean * (1.0 / 9.0)).reshape(per, 3, LEV, T)

    def co_copy(g, m):
        return rcopy(co.at[g], cb.at[per * ix + g], co_ss.at[m, g], co_rs.at[per * ix + g], 1 + ix // 2 + m, iy)

    def co_each(action):
        for m in range(half):
            for g in range(per):
                inner = jnp.logical_not(is_west) if g == 0 else jnp.logical_not(is_east)
                pl.when(inner & (1 + ix // 2 + m != ix))(lambda: action(co_copy(g, m)))

    co_each(lambda copy: copy.start())

    def put(src, g):
        for i in range(R):
            hit = a0 + g == R * ix + i
            for k in range(3):
                parent_out[k, i] = jnp.where(hit, src[k], parent_out[k, i])

    def feed(g, carry):
        j = g // per
        reach = (1 + j // 2 <= ix) & (ix <= half + j // 2)

        @pl.when(reach & (j != ix))
        def _():
            arrived(cb.at[g], co_rs.at[g])
            put(cb.at[g], g)

        @pl.when(reach & (j == ix))
        def _():
            put(co.at[lax.rem(g, per)], g)

        return carry

    lax.fori_loop(1, per * X - 1, feed, 0)

    for dx in (0, -1, 1):
        for side in (0, 1):
            pl.when(has_col[side] & row_ok(dx))(lambda: pack_copy(side, dx).wait_send())
    pl.when(ix > 0)(lambda: ph_copy(True).wait_send())
    pl.when(ix < X - 1)(lambda: ph_copy(False).wait_send())
    for j in range(H):
        pl.when(ix > 0)(lambda: halo_copy(True, j).wait_send())
        pl.when(ix < X - 1)(lambda: halo_copy(False, j).wait_send())
    pl.when(ix == half + 1)(lambda: window_copy(WEST, 3, ix - 1).wait_send())
    pl.when(ix == half - 1)(lambda: window_copy(EAST, 3, ix + 1).wait_send())
    for c in range(4):
        pl.when((ix > 0) & (ix <= half))(lambda: window_copy(WEST, c, ix - 1).wait_send())
        pl.when((ix >= half) & (ix < X - 1))(lambda: window_copy(EAST, c, ix + 1).wait_send())
    for side in (0, 1):
        pl.when(outer & has_col[side])(lambda: wt_copy(side).wait_send())
    co_each(lambda copy: copy.wait_send())


def shards(parent, nest, nest_anchor, donor_rows, donor_cols, donor_weights, wind_x, wind_y, column_mix):
    X = lax.axis_size("gx")
    CY = lax.axis_size("gz")
    Y = lax.axis_size("gy") * CY
    LEV, R = parent.shape[1], parent.shape[2]
    N, C = nest.shape[2], nest.shape[3]
    W = C + T
    top = N + 2 * H
    per = N // 3
    deep = -(-3 * LEV // T) * T
    LEVP = -(-LEV // 16) * 16
    keep = lambda x: pltpu.with_memory_space_constraint(x, pltpu.HBM)
    vmem = pl.BlockSpec(memory_space=pltpu.VMEM)
    hbm = pl.BlockSpec(memory_space=pltpu.HBM)
    smem = pl.BlockSpec(memory_space=pltpu.SMEM)
    V = lambda *s: pltpu.VMEM(s, F32)
    I = lambda *s: pltpu.VMEM(s, jnp.int32)
    D = lambda *s: pltpu.SemaphoreType.DMA(s)
    outs = pl.pallas_call(
        functools.partial(kernel, X, Y, CY),
        out_shape=(
            pltpu.VMEM((3, R, LEV, T), F32),
            pltpu.VMEM((3, N, LEV, C), F32),
        ),
        in_specs=[hbm, hbm, smem, hbm, hbm, hbm, hbm, hbm, hbm],
        out_specs=(vmem, vmem),
        scratch_shapes=[
            V(3, LEV, R, T),
            V(3, N, LEV, C),
            I(4, 2, 4, C),
            I(4, 2, 4, C),
            V(4, 2, 4, C),
            V(1, LEV),
            V(1, LEV),
            V(LEV, LEV),
            V(3, R, LEV, T),
            V(4, LEV, T),
            V(3, LEVP, deep),
            pltpu.VMEM((LEVP, deep), BF16),
            pltpu.VMEM((3, 2 * T, W), BF16),
            V(2, LEV, T),
            V(3, 2, LEV, T),
            V(2, 3, LEV, T),
            V(3, H, LEV, C),
            V(3, H, LEV, C),
            V(3, R + 2, LEV, 2 * T),
            V(3, top, LEV, W),
            V(3, top, LEV, W),
            V(2, 19, LEV, T),
            V(2, 19, LEV, T),
            V(3, 6, LEV, 2 * T),
            V(3, 4, LEV, 2 * T),
            V(2, 3, 3, 4, LEV, W),
            V(12, 4, C),
            V(2, 12, 4, T),
            V(12, 4, 8, W),
            V(3, LEV, W),
            V(4, 3, LEV, W),
            V(per, 3, LEV, T),
            V(per * X, 3, LEV, T),
            D(8),
            D(3, 2), D(3, 2), D(2), D(2), D(2, H), D(2, H), D(2, 4), D(2, 4), D(2), D(2), D(X // 2, per), D(per * X),
        ],
        compiler_params=pltpu.CompilerParams(
            collective_id=0, has_side_effects=True, vmem_limit_bytes=48 * 1024 * 1024
        ),
        cost_estimate=pl.CostEstimate(flops=200_000_000, bytes_accessed=6_000_000, transcendentals=0),
    )(
        keep(parent),
        keep(nest.transpose(0, 2, 1, 3)),
        nest_anchor,
        keep(donor_rows),
        keep(donor_cols),
        keep(donor_weights),
        keep(wind_x.reshape(1, LEV)),
        keep(wind_y.reshape(1, LEV)),
        keep(column_mix),
    )
    return tuple(x.transpose(0, 2, 1, 3) for x in outs)


def solution(mesh):
    grids = P("member", None, "gx", ("gy", "gz"))
    donors = P("member", None, None, ("gy", "gz"))
    return jax.shard_map(
        shards,
        mesh=mesh,
        in_specs=(grids, grids, P("member"), donors, donors, donors, P(), P(), P()),
        out_specs=(grids, grids),
        check_vma=False,
    )
```

```python
import functools

import jax
import jax.numpy as jnp
from jax import lax
from jax.experimental import pallas as pl
from jax.experimental.pallas import tpu as pltpu
from jax.sharding import PartitionSpec as P

MESH = pl.DeviceIdType.MESH
F32 = jnp.float32
BF16 = jnp.bfloat16
T = 128
H = 3
WEST, EAST = 0, 1


def lanes(shape, dim=1):
    return lax.broadcasted_iota(jnp.int32, shape, dim)


def split(x):
    hi = x.astype(BF16)
    lo = (x - hi.astype(F32)).astype(BF16)
    return hi, lo


def kernel(
    X, Y, CY,
    parent_in, nest_in, anchor, rows_in, cols_in, wts_in, wind_x_in, wind_y_in, mix_in,
    parent_out, nest_out,
    raw, nest, d_rows, d_cols, d_wts, wind_x, wind_y, mix, parent, coef, mixer, packed, hot,
    edge, pb, phb, hl, hh, px, sa, sb, send_w, recv_w, zb, zn, grid, wx, wrb, wxb, b0, b1, co, cb, load_s,
    pack_ss, pack_rs, ph_ss, ph_rs, halo_ss, halo_rs, win_ss, win_rs, wt_ss, wt_rs, co_ss, co_rs,
):
    pairs = (
        (nest_in, nest), (parent_in, raw), (wind_x_in, wind_x), (wind_y_in, wind_y), (mix_in, mix),
        (rows_in, d_rows), (cols_in, d_cols), (wts_in, d_wts),
    )
    loads = [pltpu.make_async_copy(a, b, load_s.at[i]) for i, (a, b) in enumerate(pairs)]
    for load in loads:
        load.start()
    R = parent.shape[1]
    N = nest.shape[1]
    LEV = nest.shape[2]
    C = nest.shape[3]
    W = C + T
    me = lax.axis_index("member")
    ix = lax.axis_index("gx")
    iy = lax.axis_index("gy") * CY + lax.axis_index("gz")
    half = X // 2
    is_west = ix == 0
    is_east = ix == X - 1
    has_col = (iy > 0, iy < Y - 1)

    def dev(x, y):
        return (me, x, y // CY, lax.rem(y, CY))

    def rcopy(src, dst, ss, rs, x, y):
        return pltpu.make_async_remote_copy(
            src_ref=src, dst_ref=dst, send_sem=ss, recv_sem=rs, device_id=dev(x, y), device_id_type=MESH
        )

    def arrived(ref, rs):
        rcopy(ref, ref, halo_ss.at[0, 0], rs, lax.rem(ix + 1, X), iy).wait_recv()

    def col_partner(side):
        return iy + (1 if side else -1)

    def row_ok(dx):
        return (ix + dx >= 0) & (ix + dx < X)

    barrier = pltpu.get_barrier_semaphore()
    for m in range(1, X):
        pl.semaphore_signal(barrier, inc=1, device_id=dev(lax.rem(ix + m, X), iy), device_id_type=MESH)
    near = jnp.int32(X - 1)
    for side in (0, 1):
        for dx in (-1, 0, 1):
            there = has_col[side] & row_ok(dx)
            near = near + there.astype(jnp.int32)

            @pl.when(there)
            def _():
                pl.semaphore_signal(
                    barrier, inc=1, device_id=dev(ix + dx, col_partner(side)), device_id_type=MESH
                )

    lane = lanes((LEV, T))
    loads[1].wait()
    for k in range(3):
        for r in range(R):
            parent[k, r] = raw[k, :, r, :]

    a0 = jnp.full((LEV, T), anchor[0], jnp.int32)
    first = (a0 - 1, a0 + (R * X // 2 - 4 - 1))
    in_west = ix <= half + 1
    in_east = ix >= half - 1

    def share_rows(which):
        base = 1 if which else 0

        def one(n, carry):
            t, k = n // 3, lax.rem(n, 3)
            body = jnp.zeros((LEV, T), F32)
            for i in range(R):
                body = jnp.where(first[which] + t == R * ix + i, parent[k, i], body)
            send_w[which, base + n] = body
            return carry

        lax.fori_loop(0, 18, one, 0)

    pl.when(in_west)(lambda: share_rows(WEST))
    pl.when(in_east)(lambda: share_rows(EAST))

    loads[0].wait()
    for side in (0, 1):
        packs = jnp.zeros((LEV, T), F32)
        for n in range(3 * N + 3 * R):
            if n < 3 * N:
                v = nest[n // N, n % N, :, C - T : C] if side else nest[n // N, n % N, :, 0:T]
                to = H * n
            else:
                m = n - 3 * N
                v = parent[m // R, m % R]
                to = 64 + H * m
            spot = (lane >= to) & (lane < to + H)
            turn = (to + H * side) % T
            packs = jnp.where(spot, pltpu.roll(v, turn, 1) if turn else v, packs)
        edge[side] = packs

    pl.semaphore_wait(barrier, near)

    def pack_copy(side, dx):
        return rcopy(
            edge.at[side], pb.at[1 - dx, 1 - side], pack_ss.at[dx + 1, side], pack_rs.at[1 - dx, 1 - side],
            ix + dx, col_partner(side),
        )

    def ph_copy(down):
        if down:
            return rcopy(parent.at[:, 0], phb.at[1], ph_ss.at[1], ph_rs.at[1], ix - 1, iy)
        return rcopy(parent.at[:, R - 1], phb.at[0], ph_ss.at[0], ph_rs.at[0], ix + 1, iy)

    def halo_copy(down, j):
        if down:
            return rcopy(nest_in.at[:, j], hh.at[:, j], halo_ss.at[1, j], halo_rs.at[1, j], ix - 1, iy)
        i = H - 1 - j
        return rcopy(nest_in.at[:, N - 1 - j], hl.at[:, i], halo_ss.at[0, j], halo_rs.at[0, j], ix + 1, iy)

    def halo_send(down, rows):
        for j in rows:
            halo_copy(down, j).start()

    spans = (((0, 6), (6, 12), (12, 15), (15, 19)), ((13, 19), (7, 13), (4, 7), (0, 4)))

    def window_copy(which, c, x):
        lo, hi = spans[which][c]
        span = pl.ds(lo, hi - lo)
        return rcopy(
            send_w.at[which, span], recv_w.at[which, span], win_ss.at[which, c], win_rs.at[which, c], x, iy
        )

    def window_add(which, c):
        window_copy(which, c, lax.rem(ix + 1, X)).wait_recv()

        def add(n, carry):
            send_w[which, n] = send_w[which, n] + recv_w[which, n]
            return carry

        lax.fori_loop(spans[which][c][0], spans[which][c][1], add, 0)

    for dx in (0, -1, 1):
        for side in (0, 1):
            there = has_col[side] & row_ok(dx)
            pl.when(there)(lambda: pack_copy(side, dx).start())
            pl.when(jnp.logical_not(there))(
                lambda: pb.__setitem__((dx + 1, side), jnp.zeros((LEV, T), F32))
            )
    pl.when(ix > 0)(lambda: ph_copy(True).start())
    pl.when(ix < X - 1)(lambda: ph_copy(False).start())
    @pl.when(ix == half)
    def _():
        for c in range(3):
            window_copy(WEST, c, ix - 1).start()
            if half < X - 1:
                window_copy(EAST, c, ix + 1).start()

    pl.when(ix > 0)(lambda: halo_send(True, (0,)))
    pl.when(ix < X - 1)(lambda: halo_send(False, (0,)))
    pl.when((ix > 0) & (ix != half) & (ix != half + 1))(lambda: halo_send(True, (1, 2)))
    pl.when((ix < X - 1) & (ix != half) & (ix != half - 1))(lambda: halo_send(False, (1, 2)))
    pl.when(ix == half)(lambda: halo_send(True, (1,)))
    pl.when((ix == half) & (ix < X - 1))(lambda: halo_send(False, (1,)))

    def pack_wait(dx):
        for side in (0, 1):
            pl.when(has_col[side] & row_ok(dx))(
                lambda: arrived(pb.at[dx + 1, side], pack_rs.at[dx + 1, side])
            )

    pack_wait(0)

    rim_spot = (lane < H) | (lane >= T - H)

    def unpack(dx, off):
        left = pltpu.roll(pb[dx + 1, 0], lax.rem(2 * T - H - off, T), 1)
        right = pltpu.roll(pb[dx + 1, 1], lax.rem(T - off, T), 1)
        return jnp.where(rim_spot, jnp.where(lane < T // 2, right, left), 0.0)

    def take_parent(n, carry):
        k, r = n // R, lax.rem(n, R)
        px[k, r + 1, :, 0:T] = parent[k, r]
        px[k, r + 1, :, T : 2 * T] = unpack(0, 64 + H * n)
        return carry

    lax.fori_loop(0, 3 * R, take_parent, 0)

    def share_rims(which):
        acc = jnp.zeros((LEV, T), F32)
        for n in range(18):
            t, k = n // 3, n % 3
            rim = jnp.zeros((LEV, T), F32)
            for i in range(R):
                rim = jnp.where(first[which] + t == R * ix + i, px[k, i + 1, :, T : 2 * T], rim)
            spot = (lane >= 6 * n) & (lane < 6 * n + 6)
            acc = jnp.where(spot, pltpu.roll(rim, (6 * n + H) % T, 1), acc)
        send_w[which, 0 if which else 18] = acc

    pl.when(in_west)(lambda: share_rims(WEST))
    pl.when(in_east)(lambda: share_rims(EAST))

    @pl.when(ix == half + 1)
    def _():
        window_copy(WEST, 3, ix - 1).start()
        halo_send(True, (1, 2))

    @pl.when(ix == half - 1)
    def _():
        window_copy(EAST, 3, ix + 1).start()
        halo_send(False, (1, 2))

    if half > 1:

        @pl.when((ix > 0) & (ix < half))
        def _():
            for c in range(3):
                window_add(WEST, c)
                window_copy(WEST, c, ix - 1).start()

    if half + 1 < X - 1:

        @pl.when((ix > half) & (ix < X - 1))
        def _():
            for c in range(3):
                window_add(EAST, c)
                window_copy(EAST, c, ix + 1).start()

    def take_rows(src, dx, first_row, count, at, only=None):
        def one(n, carry):
            k, r = (n // count, n % count) if only is not None else (n // count, lax.rem(n, count))
            sa[k, at + r, :, 0:C] = src[k, r]
            sa[k, at + r, :, C:W] = unpack(dx, H * (k * N + first_row + r))
            return carry

        if only is None:
            lax.fori_loop(0, 3 * count, one, 0)
        else:
            for k in range(3):
                one(k * count + only, 0)

    take_rows(nest, 0, 0, N, H)

    @pl.when(ix == half)
    def _():
        window_add(WEST, 3)
        window_copy(WEST, 3, ix - 1).start()
        window_add(EAST, 3)
        if half < X - 1:
            window_copy(EAST, 3, ix + 1).start()

    if half > 1:

        @pl.when((ix > 0) & (ix < half))
        def _():
            window_add(WEST, 3)
            window_copy(WEST, 3, ix - 1).start()

    if half + 1 < X - 1:

        @pl.when((ix > half) & (ix < X - 1))
        def _():
            window_add(EAST, 3)
            window_copy(EAST, 3, ix + 1).start()

    pl.when(ix == half)(lambda: halo_send(True, (2,)))
    pl.when((ix == half) & (ix < X - 1))(lambda: halo_send(False, (2,)))

    for load in loads[2:5]:
        load.wait()
    diagonal = lanes((LEV, LEV)) == lanes((LEV, LEV), 0)

    def column(ref):
        w = jnp.where(diagonal, jnp.broadcast_to(ref[...], (LEV, LEV)), 0.0)
        return jnp.broadcast_to(0.5 * jnp.sum(w, axis=1, keepdims=True), (LEV, T))

    wind = column(wind_x)
    coef[0] = 0.125 - wind
    coef[1] = 0.125 + wind
    wind = column(wind_y)
    coef[2] = 0.125 - wind
    coef[3] = 0.125 + wind
    mixer[...] = jnp.zeros_like(mixer)
    for i in range(3):
        whole = mix[...]
        top_part = whole.astype(BF16).astype(F32)
        mixer[i, 0:LEV, 0:LEV] = whole - top_part if i == 1 else top_part
    DEEP = mixer.shape[2]
    placed = mixer[0] + pltpu.roll(mixer[1], LEV, 1) + pltpu.roll(mixer[2], 2 * LEV, 1)
    packed[...] = placed.astype(BF16)
    cE, cW, cN, cS = range(4)

    def step(src, r, width):
        wide = width // T

        def cf(i):
            return jnp.concatenate([coef[i]] * wide, axis=1)

        def nb(k):
            x = src[k, r]
            return x, pltpu.roll(x, width - 1, 1), pltpu.roll(x, 1, 1)

        u, un, us = nb(0)
        v, vn, vs = nb(1)
        p, pn, ps = nb(2)

        def adv(k, x, xn, xs):
            return (
                0.5 * x + cf(cE) * src[k, r + 1] + cf(cW) * src[k, r - 1] + cf(cN) * xn + cf(cS) * xs
            )

        fu = adv(0, u, un, us) - 0.3 * (src[2, r + 1] - src[2, r - 1])
        fv = adv(1, v, vn, vs) - 0.3 * (pn - ps)
        fp = adv(2, p, pn, ps) - 0.3 * (src[0, r + 1] - src[0, r - 1] + (vn - vs))
        outs = []
        for f in (fu, fv, fp):
            hi = f.astype(BF16).astype(F32)
            stacked = jnp.concatenate([hi, hi, f - hi], axis=0)
            if DEEP > 3 * LEV:
                stacked = jnp.concatenate([stacked, jnp.zeros((DEEP - 3 * LEV, width), F32)], axis=0)
            mixed = jnp.dot(packed[...], stacked.astype(BF16), preferred_element_type=F32)
            outs.append(f + mixed[:LEV])
        return outs

    @pl.when(ix > 0)
    def _():
        arrived(phb.at[0], ph_rs.at[0])

    @pl.when(ix < X - 1)
    def _():
        arrived(phb.at[1], ph_rs.at[1])

    pl.when(ix == 0)(lambda: phb.__setitem__(0, jnp.zeros((3, LEV, T), F32)))
    pl.when(ix == X - 1)(lambda: phb.__setitem__(1, jnp.zeros((3, LEV, T), F32)))
    for k in range(3):
        px[k, 0, :, 0:T] = phb[0, k]
        px[k, R + 1, :, 0:T] = phb[1, k]
        px[k, 0, :, T : 2 * T] = jnp.zeros((LEV, T), F32)
        px[k, R + 1, :, T : 2 * T] = jnp.zeros((LEV, T), F32)

    def parent_row(r, carry):
        for k, f in enumerate(step(px, r + 1, 2 * T)):
            parent_out[k, r] = f[:, 0:T]
        return carry

    lax.fori_loop(0, R, parent_row, 0)

    def masked(f, width):
        at = lanes((1, T))
        off_left = ((at >= T // 2) & (iy == 0)) | ((at < T // 2) & (iy == Y - 1))
        tail = jnp.where(off_left, 0.0, f[:, width - T : width])
        return jnp.concatenate([f[:, 0 : width - T], tail], axis=1)

    def run(src, dst, lo, hi):
        def one(r, carry):
            for k, f in enumerate(step(src, r, W)):
                dst[k, r] = masked(f, W)
            return carry

        lax.fori_loop(lo, hi, one, 0)

    def run_out(r):
        for k, f in enumerate(step(sa, r, W)):
            nest_out[k, r - H] = f[:, 0:C]

    top = N + 2 * H
    at_w, at_e = H + 3, H + N - 4
    outer = is_west | is_east
    inner = jnp.logical_not(outer)
    run(sa, sb, jnp.where(is_west, at_w + 1, H + 1), jnp.where(is_east, at_e, H + N - 1))

    @pl.when(inner)
    def _():
        run(sb, sa, H + 2, H + N - 2)

    e = jnp.where(is_west, 0, 1)
    b_adj = jnp.where(is_west, 3, 0)

    def wt_copy(side):
        src = wx.at[:, :, C - T : C] if side else wx.at[:, :, 0:T]
        return rcopy(src, wrb.at[1 - side], wt_ss.at[side], wt_rs.at[1 - side], ix, col_partner(side))

    for load in loads[5:]:
        load.wait()

    @pl.when(outer)
    def _():
        for row in range(4):
            for dc in range(3):
                acc = jnp.zeros((4, C), F32)
                for n in range(4):
                    hit = (d_rows[n, e] == row) & (d_cols[n, e] == dc - 1)
                    acc = acc + jnp.where(hit, d_wts[n, e], 0.0)
                wx[row * 3 + dc] = acc
        for side in (0, 1):
            pl.when(has_col[side])(lambda: wt_copy(side).start())
            pl.when(jnp.logical_not(has_col[side]))(
                lambda: wrb.__setitem__(side, jnp.zeros((12, 4, T), F32))
            )

    def take(j, low):
        if low:
            arrived(hl.at[:, H - 1 - j], halo_rs.at[0, j])
            take_rows(hl, -1, N - H, H, 0, H - 1 - j)
        else:
            arrived(hh.at[:, j], halo_rs.at[1, j])
            take_rows(hh, 1, 0, H, H + N, j)

    def at(j, s, low):
        return H - j + s - 1 if low else H + N - 1 + j - s + 1

    def one_row(src, dst, r):
        run(src, dst, r, r + 1)

    def grow(j, low):
        one_row(sa, sb, at(j, 1, low))
        one_row(sb, sa, at(j, 2, low))
        run_out(at(j, 3, low))

    @pl.when(ix > 0)
    def _():
        pack_wait(-1)
        take(0, True)
        one_row(sa, sb, at(0, 1, True))

    @pl.when(ix < X - 1)
    def _():
        pack_wait(1)
        take(0, False)
        one_row(sa, sb, at(0, 1, False))

    @pl.when(outer)
    def _():
        for side in (0, 1):
            pl.when(has_col[side])(lambda: arrived(wrb.at[side], wt_rs.at[side]))
        at8 = lanes((8, T))
        for b in range(4):
            for i in range(12):
                left = jnp.broadcast_to(wrb[0, i, b : b + 1, :], (8, T))
                right = jnp.broadcast_to(wrb[1, i, b : b + 1, :], (8, T))
                wxb[i, b, :, 0:C] = jnp.broadcast_to(wx[i, b : b + 1, :], (8, C))
                wxb[i, b, :, C:W] = jnp.where(at8 < T // 2, right, left)

        y = lanes((2 * T, W))
        c = lanes((2 * T, W), 0)
        y = jnp.where(y < C + T // 2, y, y - W)
        c = jnp.where(c < T + T // 2, c, c - 2 * T)
        for dc in range(3):
            gap = y - 3 * (c - (dc - 1))
            hot[dc] = jnp.where((gap >= 0) & (gap <= 2), 1.0, 0.0).astype(BF16)

    def edge_work(which):
        base = 1 if which else 0
        rims = 0 if which else 18
        for c in range(4):
            window_add(which, c)

        def lay(n, carry):
            t, k = n // 3, lax.rem(n, 3)
            zb[k, t, :, 0:T] = send_w[which, base + n]
            tail = pltpu.roll(send_w[which, rims], lax.rem(2 * T - 6 * n - H, T), 1)
            zb[k, t, :, T : 2 * T] = jnp.where(rim_spot, tail, 0.0)
            return carry

        lax.fori_loop(0, 18, lay, 0)

    pl.when(is_west)(lambda: edge_work(WEST))
    pl.when(is_east)(lambda: edge_work(EAST))

    @pl.when(outer)
    def _():
        def zone_row(r, carry):
            for k, f in enumerate(step(zb, r + 1, 2 * T)):
                zn[k, r] = masked(f, 2 * T)
            return carry

        lax.fori_loop(0, 4, zone_row, 0)
        for dc in range(3):

            def spread(k, carry):
                for time in range(2):
                    rows = zn[k] if time else zb[k, 1:5]
                    hi, lo = split(rows.reshape(4 * LEV, 2 * T))
                    got = jnp.dot(hi, hot[dc], preferred_element_type=F32) + jnp.dot(
                        lo, hot[dc], preferred_element_type=F32
                    )
                    grid[time, k, dc] = got.reshape(4, LEV, W)
                return carry

            lax.fori_loop(0, 3, spread, 0)

        def bound(time, k, b):
            acc = jnp.zeros((LEV, W), F32)
            for row in range(4):
                for dc in range(3):
                    w = jnp.concatenate([wxb[row * 3 + dc, b]] * (LEV // 8), axis=0)
                    acc = acc + w * grid[time, k, dc, row]
            return acc

        def each(n, carry):
            k, b = n // 4, lax.rem(n, 4)
            got = bound(1, k, b)
            b1[b, k] = got
            nest_out[k, jnp.where(is_west, 0, N - 4) + b] = got[:, 0:C]
            return carry

        lax.fori_loop(0, 12, each, 0)

        def each0(k, carry):
            b0[k] = bound(0, k, b_adj)
            return carry

        lax.fori_loop(0, 3, each0, 0)

        ra = jnp.where(is_west, at_w, at_e)
        for k in range(3):
            sb[k, ra] = (1.0 - 1.0 / 3.0) * b0[k] + (1.0 / 3.0) * b1[b_adj, k]
            sa[k, ra] = (1.0 - 2.0 / 3.0) * b0[k] + (2.0 / 3.0) * b1[b_adj, k]

    @pl.when(ix > 0)
    def _():
        one_row(sb, sa, at(0, 2, True))
        pl.when(inner)(lambda: run_out(at(0, 3, True)))

    @pl.when(ix < X - 1)
    def _():
        one_row(sb, sa, at(0, 2, False))
        pl.when(inner)(lambda: run_out(at(0, 3, False)))

    for low in (True, False):

        @pl.when(ix > 0 if low else ix < X - 1)
        def _():
            for j in (1, 2):
                take(j, low)
                grow(j, low)

    per = N // 3
    sums = []
    for g in range(per):
        for k in range(3):
            sums.append(nest_out[k, 3 * g] + nest_out[k, 3 * g + 1] + nest_out[k, 3 * g + 2])
    hi, lo = split(jnp.concatenate(sums, axis=0))
    gap = lanes((C, T), 0) - 3 * lanes((C, T))
    pool = jnp.where((gap >= 0) & (gap <= 2), 1.0, 0.0).astype(BF16)
    mean = jnp.dot(hi, pool, preferred_element_type=F32) + jnp.dot(lo, pool, preferred_element_type=F32)
    co[...] = (mean * (1.0 / 9.0)).reshape(per, 3, LEV, T)

    def co_copy(g, m):
        return rcopy(co.at[g], cb.at[per * ix + g], co_ss.at[m, g], co_rs.at[per * ix + g], 1 + ix // 2 + m, iy)

    def co_each(action):
        for m in range(half):
            for g in range(per):
                inner = jnp.logical_not(is_west) if g == 0 else jnp.logical_not(is_east)
                pl.when(inner & (1 + ix // 2 + m != ix))(lambda: action(co_copy(g, m)))

    co_each(lambda copy: copy.start())

    def put(src, g):
        for i in range(R):
            hit = a0 + g == R * ix + i
            for k in range(3):
                parent_out[k, i] = jnp.where(hit, src[k], parent_out[k, i])

    def feed(g, carry):
        j = g // per
        reach = (1 + j // 2 <= ix) & (ix <= half + j // 2)

        @pl.when(reach & (j != ix))
        def _():
            arrived(cb.at[g], co_rs.at[g])
            put(cb.at[g], g)

        @pl.when(reach & (j == ix))
        def _():
            put(co.at[lax.rem(g, per)], g)

        return carry

    lax.fori_loop(1, per * X - 1, feed, 0)

    for dx in (0, -1, 1):
        for side in (0, 1):
            pl.when(has_col[side] & row_ok(dx))(lambda: pack_copy(side, dx).wait_send())
    pl.when(ix > 0)(lambda: ph_copy(True).wait_send())
    pl.when(ix < X - 1)(lambda: ph_copy(False).wait_send())
    for j in range(H):
        pl.when(ix > 0)(lambda: halo_copy(True, j).wait_send())
        pl.when(ix < X - 1)(lambda: halo_copy(False, j).wait_send())
    pl.when(ix == half + 1)(lambda: window_copy(WEST, 3, ix - 1).wait_send())
    pl.when(ix == half - 1)(lambda: window_copy(EAST, 3, ix + 1).wait_send())
    for c in range(4):
        pl.when((ix > 0) & (ix <= half))(lambda: window_copy(WEST, c, ix - 1).wait_send())
        pl.when((ix >= half) & (ix < X - 1))(lambda: window_copy(EAST, c, ix + 1).wait_send())
    for side in (0, 1):
        pl.when(outer & has_col[side])(lambda: wt_copy(side).wait_send())
    co_each(lambda copy: copy.wait_send())


def shards(parent, nest, nest_anchor, donor_rows, donor_cols, donor_weights, wind_x, wind_y, column_mix):
    X = lax.axis_size("gx")
    CY = lax.axis_size("gz")
    Y = lax.axis_size("gy") * CY
    LEV, R = parent.shape[1], parent.shape[2]
    N, C = nest.shape[2], nest.shape[3]
    W = C + T
    top = N + 2 * H
    per = N // 3
    deep = -(-3 * LEV // T) * T
    LEVP = -(-LEV // 16) * 16
    keep = lambda x: pltpu.with_memory_space_constraint(x, pltpu.HBM)
    vmem = pl.BlockSpec(memory_space=pltpu.VMEM)
    hbm = pl.BlockSpec(memory_space=pltpu.HBM)
    smem = pl.BlockSpec(memory_space=pltpu.SMEM)
    V = lambda *s: pltpu.VMEM(s, F32)
    I = lambda *s: pltpu.VMEM(s, jnp.int32)
    D = lambda *s: pltpu.SemaphoreType.DMA(s)
    outs = pl.pallas_call(
        functools.partial(kernel, X, Y, CY),
        out_shape=(
            pltpu.VMEM((3, R, LEV, T), F32),
            pltpu.VMEM((3, N, LEV, C), F32),
        ),
        in_specs=[hbm, hbm, smem, hbm, hbm, hbm, hbm, hbm, hbm],
        out_specs=(vmem, vmem),
        scratch_shapes=[
            V(3, LEV, R, T),
            V(3, N, LEV, C),
            I(4, 2, 4, C),
            I(4, 2, 4, C),
            V(4, 2, 4, C),
            V(1, LEV),
            V(1, LEV),
            V(LEV, LEV),
            V(3, R, LEV, T),
            V(4, LEV, T),
            V(3, LEVP, deep),
            pltpu.VMEM((LEVP, deep), BF16),
            pltpu.VMEM((3, 2 * T, W), BF16),
            V(2, LEV, T),
            V(3, 2, LEV, T),
            V(2, 3, LEV, T),
            V(3, H, LEV, C),
            V(3, H, LEV, C),
            V(3, R + 2, LEV, 2 * T),
            V(3, top, LEV, W),
            V(3, top, LEV, W),
            V(2, 19, LEV, T),
            V(2, 19, LEV, T),
            V(3, 6, LEV, 2 * T),
            V(3, 4, LEV, 2 * T),
            V(2, 3, 3, 4, LEV, W),
            V(12, 4, C),
            V(2, 12, 4, T),
            V(12, 4, 8, W),
            V(3, LEV, W),
            V(4, 3, LEV, W),
            V(per, 3, LEV, T),
            V(per * X, 3, LEV, T),
            D(8),
            D(3, 2), D(3, 2), D(2), D(2), D(2, H), D(2, H), D(2, 4), D(2, 4), D(2), D(2), D(X // 2, per), D(per * X),
        ],
        compiler_params=pltpu.CompilerParams(
            collective_id=0, has_side_effects=True, vmem_limit_bytes=48 * 1024 * 1024
        ),
        cost_estimate=pl.CostEstimate(flops=200_000_000, bytes_accessed=6_000_000, transcendentals=0),
    )(
        keep(parent),
        keep(nest.transpose(0, 2, 1, 3)),
        nest_anchor,
        keep(donor_rows),
        keep(donor_cols),
        keep(donor_weights),
        keep(wind_x.reshape(1, LEV)),
        keep(wind_y.reshape(1, LEV)),
        keep(column_mix),
    )
    return tuple(x.transpose(0, 2, 1, 3) for x in outs)


def solution(mesh):
    grids = P("member", None, "gx", ("gy", "gz"))
    donors = P("member", None, None, ("gy", "gz"))
    return jax.shard_map(
        shards,
        mesh=mesh,
        in_specs=(grids, grids, P("member"), donors, donors, donors, P(), P(), P()),
        out_specs=(grids, grids),
        check_vma=False,
    )
```
